32 devices in a mesh: pair: 8 (over z, x), aux: 4 (over y, core).
Axes of the slice: x: 2, y: 2, z: 4, core: 2. Of those that a mesh axis runs over, the one named last changes fastest.
Arguments:
- factor: float32 [131072, 4096], P('pair', 'aux'), may hold values from -0.015625 to 0.015625
- trials: float32 [256, 131072], P('aux', 'pair'), may hold values from -6 to 6
- stored: float32 [384, 131072], P(None, 'pair'), may hold values from -0.015625 to 0.015625
- energy_gaps: float32 [131072], P('pair'), may hold values from 0.35 to 7
Outputs:
- next_trials: float32 [256, 131072], P('aux', 'pair')
- projections: float32 [2, 384, 256], P(None, None, 'aux')
The draws below stay inside these ranges and needn't reach their ends.
All inputs are finite; a program needn't handle non-finite values.
Results may differ from the reference program's by a relative error of at most 0.0001.
Values sent between devices are 32-bit elements; how exact they have to be, the bound alone decides.
No kernel may reach another device: no remote copies, remote signals or barrier semaphores. Data moves between devices by JAX's collectives and lax.ppermute only.
A program may use at most 192 MiB of HBM per device.

```python
import jax
import jax.numpy as jnp
from jax import lax

PAIRS = 131072
AUX = 4096
STORED = 384
ROUNDS = 2
TRIALS = 256


def draw_energy_gaps(key, part):
    ramp = jnp.arange(PAIRS, dtype=jnp.float32) / PAIRS
    jitter = jax.random.uniform(jax.random.fold_in(key, 7), (PAIRS,), jnp.float32, 0.7, 1.4)
    return (0.5 + 4.5 * ramp) * jitter


def shard_levels(own_key, extent, pieces, smallest, largest):
    loudness = 1.0
    for position, parts in pieces:
        heights = jax.random.uniform(jax.random.fold_in(jax.random.fold_in(own_key, 6), position), (parts,), jnp.float32, smallest / len(pieces), largest / len(pieces))
        loudness = loudness * jnp.repeat(jnp.exp(heights), extent[position] // parts).reshape((-1,) + (1,) * (len(extent) - 1 - position))
    return loudness


def noise(key, dims, scale, bound, shards=(), held_as=jnp.bfloat16):
    array = jax.random.normal(key, dims, jnp.float32) * scale
    if len(shards) > 0:
        array = shard_levels(key, dims, shards, -0.22, 0.18) * array
    return jnp.clip(array, min=-bound, max=bound).astype(held_as)


def setup_inputs(seed: int = 0) -> dict:
    keys = jax.random.split(jax.random.key(seed), 5)
    factor = noise(keys[0], (PAIRS, AUX), PAIRS ** -0.5, 0.015625, ((0, 8), (1, 4)), jnp.float32)
    trials = noise(keys[1], (TRIALS, PAIRS), 1.0, 6.0, ((0, 4), (1, 8)), jnp.float32)
    stored = noise(keys[2], (STORED, PAIRS), PAIRS ** -0.5, 0.015625, ((1, 8),), jnp.float32)
    energy_gaps = draw_energy_gaps(jax.random.fold_in(keys[4], 71), 0)
    return dict(factor=factor, trials=trials, stored=stored, energy_gaps=energy_gaps)


def reference(factor, trials, stored, energy_gaps):
    highest = lax.Precision.HIGHEST
    current = trials
    collected = []
    for turn_index in range(ROUNDS):
        fitted = jnp.dot(current, factor, precision=highest, preferred_element_type=jnp.float32)
        coulomb = lax.dot_general(fitted, factor, (((1,), (1,)), ((), ())), precision=highest, preferred_element_type=jnp.float32)
        response = energy_gaps[None, :] * current + 4.0 * coulomb
        projection = lax.dot_general(stored, response, (((1,), (1,)), ((), ())), precision=highest, preferred_element_type=jnp.float32)
        removed = lax.dot_general(projection, stored, (((0,), (0,)), ((), ())), precision=highest, preferred_element_type=jnp.float32)
        remainder = response - removed
        scaled = remainder / energy_gaps[None, :]
        row_norm = jnp.sqrt(lax.optimization_barrier(jnp.mean(scaled * scaled, axis=1, keepdims=True)) + 1e-06)
        current = scaled / row_norm
        collected.append(projection)
    return (current, jnp.stack(collected))
```

```python
import functools

import jax
import jax.numpy as jnp
from jax import lax
from jax.experimental import pallas as pl
from jax.experimental.pallas import tpu as pltpu
from jax.sharding import PartitionSpec as P

ROUNDS = 2
PIECES = 4
VMEM = 56 * 1024 * 1024
NN = (((1,), (0,)), ((), ()))
NT = (((1,), (1,)), ((), ()))


def split(x):
    hi = x.astype(jnp.bfloat16)
    lo = (x - hi.astype(jnp.float32)).astype(jnp.bfloat16)
    return hi, lo


def dot(a, b, dims):
    return lax.dot_general(a, b, dims, preferred_element_type=jnp.float32)


def dot3(a_both, b, dims):
    rows = a_both.shape[0] // 2
    b_hi, b_lo = b
    both = dot(a_both, b_hi, dims)
    return both[:rows] + both[rows:] + dot(a_both[:rows], b_lo, dims)


def block_of(size, most):
    block = size
    while block > most and block % 2 == 0:
        block //= 2
    return block


def light():
    return pl.CostEstimate(flops=1, bytes_accessed=1, transcendentals=0)


def pass_over(factor, chunk, columns, fitted=None, parts=None, gaps=None, stored=None, which=None, before=None, after=(), pieces=PIECES, most=2048):
    aux = factor.shape[1]
    block = block_of(columns, most)
    steps = columns // block
    first = chunk * steps
    out_rows = fitted.shape[0] if fitted is not None else 0
    half = out_rows // 2
    piece = half // pieces
    wide = gaps is not None
    own = extra = 0
    if wide:
        own = stored.shape[0] // which[1]
        extra = -(-own // 128) * 128
    parts = parts or []
    rows = sum(p.shape[0] for p in parts)
    after = [a for a in after if a is not None]

    def kernel(*refs):
        refs = list(refs)
        if wide:
            refs.pop(0)
        f_ref = refs.pop(0)
        if half:
            t_ref = refs.pop(0)
        xs = [refs.pop(0) for _ in parts]
        if wide:
            g_ref, s_ref = refs.pop(0), refs.pop(0)
        b_ref = refs.pop(0) if before is not None else None
        for _ in after:
            refs.pop(0)
        if half:
            keep_ref = refs.pop(0)
            send_refs = [refs.pop(0) for _ in range(pieces)]
        o_ref = refs.pop(0) if parts else None
        if half:
            both_ref = refs.pop(0)

        @pl.when(pl.program_id(0) == 0)
        def _():
            if half:
                hi, lo = split(4.0 * t_ref[...])
                both_ref[:out_rows] = hi
                both_ref[out_rows:] = lo
            if parts:
                if b_ref is None:
                    o_ref[...] = jnp.zeros_like(o_ref)
                else:
                    o_ref[...] = b_ref[...]

        factors = split(f_ref[...])
        if half:
            out = dot3(both_ref[...], factors, NT)
            keep_ref[...] = out[:half]
            for i, r in enumerate(send_refs):
                r[...] = out[half + i * piece : half + (i + 1) * piece]
        if parts:
            x = jnp.concatenate([r[...] for r in xs], axis=0) if len(xs) > 1 else xs[0][...]
            o_ref[:, :aux] += dot3(jnp.concatenate(split(x), axis=0), factors, NN)
            if wide:
                both = jnp.concatenate(split(x * g_ref[...]), axis=0)
                o_ref[:, aux : aux + own] += dot3(both, split(s_ref[...]), NT)

    in_specs = [pl.BlockSpec((block, aux), lambda k, *_: (first + k, 0))]
    args = [factor]
    if half:
        in_specs.append(pl.BlockSpec((out_rows, aux), lambda k, *_: (0, 0)))
        args.append(fitted)
    for p in parts:
        offset = first if p.shape[1] != columns else 0
        in_specs.append(pl.BlockSpec((p.shape[0], block), lambda k, *_, offset=offset: (0, offset + k)))
        args.append(p)
    if wide:
        in_specs.append(pl.BlockSpec((1, block), lambda k, *_: (0, first + k)))
        in_specs.append(pl.BlockSpec((own, block), lambda k, a: (a[0], first + k)))
        args += [gaps, stored]
    if before is not None:
        in_specs.append(pl.BlockSpec(before.shape, lambda k, *_: (0, 0)))
        args.append(before)
    for a in after:
        in_specs.append(pl.BlockSpec(memory_space=pl.ANY))
        args.append(a)
    shapes, specs = [], []
    if half:
        for height in [half] + [piece] * pieces:
            shapes.append(jax.ShapeDtypeStruct((height, columns), jnp.float32))
            specs.append(pl.BlockSpec((height, block), lambda k, *_: (0, k)))
    if parts:
        shapes.append(jax.ShapeDtypeStruct((rows, aux + extra), jnp.float32))
        specs.append(pl.BlockSpec((rows, aux + extra), lambda k, *_: (0, 0)))
    if wide:
        args = [which[0]] + args
    out = pl.pallas_call(
        kernel,
        out_shape=tuple(shapes),
        grid_spec=pltpu.PrefetchScalarGridSpec(
            num_scalar_prefetch=1 if wide else 0,
            grid=(steps,),
            in_specs=in_specs,
            out_specs=tuple(specs),
            scratch_shapes=[pltpu.VMEM((2 * out_rows, aux), jnp.bfloat16)] if half else [],
        ),
        compiler_params=pltpu.CompilerParams(vmem_limit_bytes=VMEM),
        cost_estimate=light(),
        name=("spread" if half else "") + ("fit" if parts else ""),
    )(*args)
    if half:
        out = [out[0], list(out[1 : 1 + pieces]), *out[1 + pieces :]]
    return out


def assemble(summed, arrived, olds, old_chunks, projection, stored, gaps, chunk, swap, after=(), most=2048):
    rows, columns = arrived.shape
    total = stored.shape[0]
    block = block_of(columns, most)
    steps = columns // block
    first = chunk * steps
    half = rows // 2
    pieces = PIECES if swap else 1
    piece = rows // pieces

    def kernel(*refs):
        refs = list(refs)
        c_ref, y_ref = refs.pop(0), refs.pop(0)
        xs = [refs.pop(0) for _ in olds]
        p_ref, s_ref, g_ref = refs[:3]
        o_refs, q_ref = refs[-1 - pieces : -1], refs[-1]
        arrival = y_ref[...]
        if swap:
            arrival = jnp.concatenate([arrival[half:], arrival[:half]], axis=0)
        x = jnp.concatenate([r[...] for r in xs], axis=0) if len(xs) > 1 else xs[0][...]
        both = jnp.concatenate(split(p_ref[...]), axis=0)
        removed = dot3(both, split(s_ref[...]), NN)
        new = x + (c_ref[...] + arrival - removed) / g_ref[...]
        for i, r in enumerate(o_refs):
            r[...] = new[i * piece : (i + 1) * piece]

        @pl.when(pl.program_id(0) == 0)
        def _():
            q_ref[...] = jnp.zeros_like(q_ref)

        q_ref[...] += jnp.sum(new * new, axis=1, keepdims=True)

    def old_spec(height, offset):
        return pl.BlockSpec((height, block), lambda k: (0, offset * steps + k))

    in_specs = [
        pl.BlockSpec((rows, block), lambda k: (0, k)),
        pl.BlockSpec((rows, block), lambda k: (0, k)),
    ]
    share = rows // len(olds)
    in_specs += [old_spec(share, c) for c in old_chunks]
    in_specs += [
        pl.BlockSpec((rows, total), lambda k: (0, 0)),
        pl.BlockSpec((total, block), lambda k: (0, first + k)),
        pl.BlockSpec((1, block), lambda k: (0, first + k)),
    ]
    in_specs += [pl.BlockSpec(memory_space=pl.ANY) for _ in after]
    *new, squares = pl.pallas_call(
        kernel,
        out_shape=(
            *[jax.ShapeDtypeStruct((piece, columns), jnp.float32)] * pieces,
            jax.ShapeDtypeStruct((rows, 128), jnp.float32),
        ),
        grid=(steps,),
        in_specs=in_specs,
        out_specs=(
            *[pl.BlockSpec((piece, block), lambda k: (0, k))] * pieces,
            pl.BlockSpec((rows, 128), lambda k: (0, 0)),
        ),
        compiler_params=pltpu.CompilerParams(vmem_limit_bytes=VMEM),
        cost_estimate=light(),
        name="assemble",
    )(summed, arrived, *olds, projection, stored, gaps, *after)
    return new, squares


def swap_with(value, axis, size, distance):
    return lax.ppermute(value, axis, [(i, i ^ distance) for i in range(size)])


def small(kernel, shapes, *args, name="small", scalar=None, after=()):
    out = tuple(jax.ShapeDtypeStruct(x, jnp.float32) for x in shapes)
    specs = [pl.BlockSpec(memory_space=pltpu.VMEM)] * len(args)
    if scalar is not None:
        specs = [pl.BlockSpec(memory_space=pltpu.SMEM)] + specs
        args = (scalar, *args)
    used = len(args)

    def body(*refs):
        kernel(*refs[:used], *refs[used + len(after) :])

    specs += [pl.BlockSpec(memory_space=pl.ANY)] * len(after)
    args = (*args, *after)
    return pl.pallas_call(
        body,
        out_shape=out,
        in_specs=specs,
        out_specs=tuple(pl.BlockSpec(memory_space=pltpu.VMEM) for _ in out),
        compiler_params=pltpu.CompilerParams(vmem_limit_bytes=VMEM // 2),
        cost_estimate=light(),
        name=name,
    )(*args)


def total_of(*values, after=()):
    def kernel(*refs):
        acc = refs[0][...]
        for r in refs[1:-1]:
            acc = acc + r[...]
        refs[-1][...] = acc

    return small(kernel, [values[0].shape], *values, name="total", after=after)[0]


def joined(keep, near, parts, after=(), most=4096):
    rows, columns = keep.shape
    block = block_of(columns, most)
    each = near[0].shape[0]
    height = rows // parts

    def kernel(k_ref, *refs):
        ins, outs = refs[: len(near)], refs[len(near) + len(after) :]
        for i, r in enumerate(ins):
            at = i * each
            outs[at // height][at % height : at % height + each] = k_ref[at : at + each] + r[...]

    return pl.pallas_call(
        kernel,
        out_shape=tuple([jax.ShapeDtypeStruct((height, columns), jnp.float32)] * parts),
        grid=(columns // block,),
        in_specs=[pl.BlockSpec((rows, block), lambda k: (0, k))]
        + [pl.BlockSpec((each, block), lambda k: (0, k))] * len(near)
        + [pl.BlockSpec(memory_space=pl.ANY)] * len(after),
        out_specs=tuple([pl.BlockSpec((height, block), lambda k: (0, k))] * parts),
        compiler_params=pltpu.CompilerParams(vmem_limit_bytes=VMEM),
        cost_estimate=light(),
        name="joined",
    )(keep, *near, *after)


def pair_sum(value, size, columns=None, between=(None, None)):
    rows = value.shape[0]
    columns = columns or value.shape[1]
    block = rows // 4
    me = jnp.reshape(lax.axis_index("pair") % 4, (1,)).astype(jnp.int32)

    def cut(m_ref, v_ref, *out):
        for d, o in enumerate(out):
            o[...] = v_ref[pl.ds(pl.multiple_of((m_ref[0] ^ d) * block, 8), block), :columns]

    def gather(m_ref, *refs):
        for d, r in enumerate(refs[:-1]):
            refs[-1][pl.ds(pl.multiple_of((m_ref[0] ^ d) * block, 8), block), :] = r[...]

    mine, *rest = small(cut, [(block, columns)] * 4, value, scalar=me, name="cut")
    others = [swap_with(r, "pair", size, d) for d, r in enumerate(rest, 1)]
    after = [between[0]([mine])] if between[0] else []
    total = total_of(mine, *others, after=after)
    distance = 4
    while distance < size:
        other = swap_with(total, "pair", size, distance)
        after = [between[1]([total])] if between[1] and distance == 4 else []
        total = total_of(total, other, after=after)
        distance *= 2
    every = [total] + [swap_with(total, "pair", size, d) for d in (1, 2, 3)]
    return small(gather, [(rows, columns)], *every, scalar=me, name="gather")[0]


def small_sum(value, size):
    if size & (size - 1):
        return lax.psum(value, "pair")
    distance = 1
    while distance < size:
        value = value + swap_with(value, "pair", size, distance)
        distance *= 2
    return value


def on_device(n_pair, n_aux, factor, trials, stored, energy_gaps):
    local, aux = factor.shape
    total = stored.shape[0]
    pairs = local * n_pair
    owned = trials.shape[0]
    own_s = total // n_aux
    me = lax.axis_index("aux")
    which = (jnp.reshape(me, (1,)).astype(jnp.int32), n_aux)
    gaps = energy_gaps[None, :]
    chunks = 2
    h = owned // 2
    two = 2 * h
    kc = local // chunks
    aux_swap = functools.partial(swap_with, axis="aux", size=n_aux)
    over = functools.partial(pass_over, factor)
    wide = dict(gaps=gaps, stored=stored, which=which)

    def project(fitted, partial, crossed):
        def part(m_ref, f_ref, p_ref, w_ref, keep_ref, send_ref):
            f = jnp.concatenate(split(4.0 * f_ref[...]), axis=0)
            own = p_ref[:, aux:]
            shape = (own.shape[1], total)
            row = lax.broadcasted_iota(jnp.int32, shape, 0)
            column = lax.broadcasted_iota(jnp.int32, shape, 1)
            here = (column == row + m_ref[0] * own_s) & (row < own_s)
            here = jnp.where(here, 1.0, 0.0).astype(jnp.bfloat16)
            placed = dot(jnp.concatenate(split(own), axis=0), here, NN)
            rows = own.shape[0]
            out = dot3(f, split(w_ref[...]), NT) + placed[:rows] + placed[rows:]
            keep_ref[...] = out[:two]
            send_ref[...] = out[two:]

        def both(k_ref, t_ref, o_ref):
            o_ref[:h] = k_ref[:h] + t_ref[h:]
            o_ref[h:] = k_ref[h:] + t_ref[:h]

        keep, send = small(part, [(two, total)] * 2, fitted, partial, crossed, scalar=which[0], name="project")
        first_part = keep
        keep = total_of(keep, aux_swap(send, distance=1))
        part_sum = small(both, [(two, total)], keep, aux_swap(keep, distance=2), name="both")[0]
        return first_part, part_sum, pair_sum(part_sum, n_pair)

    everyone = []
    for g in range(2):
        per_chunk = []
        for c in range(chunks):
            own = trials[g * h : (g + 1) * h, c * kc : (c + 1) * kc]
            per_chunk.append([own, aux_swap(own, distance=2)])
        everyone.append(per_chunk)

    def near_too(parts, token):
        parts = lax.optimization_barrier((*parts, token))[:2]
        return [*parts, *(aux_swap(p, distance=1) for p in parts)]

    crossed = None
    quarter = local // 4
    for c in range(2):
        (crossed,) = over(c, quarter, parts=[stored], before=crossed, after=[crossed])
    partial = None
    for c in range(chunks):
        everyone[0][c] = near_too(everyone[0][c], crossed)
        (partial,) = over(c, kc, parts=everyone[0][c], before=partial, **wide)
    held = [crossed]

    def more(c):
        def run(after):
            held.extend(over(c, quarter, parts=[stored], before=held[-1], after=after))
            return held[-1]

        return run

    one_part = partial
    one = pair_sum(partial, n_pair, aux, (more(2), more(3)))
    crossed = held[-1]

    def summed(keep, send, after):
        (keep,) = joined(keep, [aux_swap(x, distance=1) for x in send], 1, after)
        return keep, aux_swap(keep, distance=2)

    def new_vectors(g, c, pair, projection, token):
        new, square = assemble(
            *pair, everyone[g][c][:2], (0, 0), projection, stored, gaps, c, True, after=token
        )
        return new + [aux_swap(x, distance=1) for x in new], square[:h]

    begun, aux_sum, first = project(one, one_part, crossed)
    projected = [[None, None], [None, None]]
    projected[0][0] = first[:h]
    partial, sent, token = None, [[], []], [crossed, begun]
    for c in range(chunks):
        everyone[1][c] = near_too(everyone[1][c], crossed)
        keep, send, partial = over(c, kc, fitted=one, parts=everyone[1][c], before=partial, after=token, **wide)
        sent[0].append(summed(keep, send, [aux_sum]))
        token = [sent[0][-1][0]]
    two_part = partial
    two_sum = pair_sum(partial, n_pair, aux)
    current = [[], []]
    squares = [0.0, 0.0]
    begun, aux_sum, second = project(two_sum, two_part, crossed)
    projected[0][1] = second[:h]

    partial, token = None, [two_sum, sent[0][-1][0]]
    for c in range(chunks):
        x, square = new_vectors(0, c, sent[0][c], first, token)
        current[0].append(x)
        squares[0] = squares[0] + square
        keep, send, partial = over(c, kc, fitted=two_sum, parts=x, before=partial, after=[begun], **wide)
        sent[1].append(summed(keep, send, [aux_sum]))
        token = [sent[1][-1][0]]
    one_part = partial
    one = pair_sum(partial, n_pair, aux)
    begun, aux_sum, first = project(one, one_part, crossed)
    first = first[:h]
    projected[1][0] = first

    def last_sum(keep, send, after):
        near = [aux_swap(x, distance=1) for x in send]
        own, far = joined(keep, near, 2, after)
        return own, aux_swap(far, distance=2)

    partial, last = None, [[], []]
    for c in range(chunks):
        x, square = new_vectors(1, c, sent[1][c], second, token)
        current[1].append(x)
        squares[1] = squares[1] + square
        if c == 0:
            keep, send, partial = over(c, kc, fitted=one, parts=x, before=partial, after=[begun], **wide)
            last[0].append(last_sum(keep, send, [aux_sum]))
            keep, send = over(c + 1, kc, fitted=one, after=[last[0][-1][0]])
            last[0].append(last_sum(keep, send, []))
            token = [last[0][-1][0]]
        else:
            (partial,) = over(c, kc, parts=x, before=partial, **wide)
    ends = [[], []]
    norms = [0.0, 0.0]

    def finish(g, c, projection, token):
        new, square = assemble(
            *last[g][c],
            current[g][c][: PIECES // 2],
            (0,) * (PIECES // 2),
            projection,
            stored,
            gaps,
            c,
            False,
            after=token,
        )
        ends[g].append(new[0])
        norms[g] = norms[g] + square
        return new[0]

    two_part = partial
    two_sum = pair_sum(
        partial,
        n_pair,
        aux,
        (lambda after: finish(0, 0, first, after), lambda after: finish(0, 1, first, after)),
    )
    begun, aux_sum, second = project(two_sum, two_part, crossed)
    second = second[:h]
    projected[1][1] = second
    token = [begun]
    for c in range(chunks):
        keep, send = over(c, kc, fitted=two_sum, after=token, pieces=2 * PIECES)
        last[1].append(last_sum(keep, send, [aux_sum]))
        token = [last[1][-1][0]]
    token = []
    for c in range(chunks):
        token = [finish(1, c, second, token)]

    sums = jnp.concatenate([jnp.concatenate(squares, 0), jnp.concatenate(norms, 0)], axis=1)
    sums = small_sum(sums, n_pair)
    norm = jnp.sqrt(sums[:, :1] / pairs + 1e-06)
    scale = norm * jnp.sqrt(sums[:, 128:129] / (norm * norm) / pairs + 1e-06)
    out = jnp.concatenate([jnp.concatenate(e, axis=1) for e in ends], axis=0) / scale
    first_p = jnp.concatenate(projected[0], axis=0)
    second_p = jnp.concatenate(projected[1], axis=0) / norm
    return out, jnp.stack([first_p.T, second_p.T])


def solution(mesh):
    in_specs = (P("pair", "aux"), P("aux", "pair"), P(None, "pair"), P("pair"))
    out_specs = (P("aux", "pair"), P(None, None, "aux"))
    body = functools.partial(on_device, mesh.shape["pair"], mesh.shape["aux"])
    return jax.shard_map(body, mesh=mesh, in_specs=in_specs, out_specs=out_specs, check_vma=False)
```

```python
import functools

import jax
import jax.numpy as jnp
from jax import lax
from jax.experimental import pallas as pl
from jax.experimental.pallas import tpu as pltpu
from jax.sharding import PartitionSpec as P

ROUNDS = 2
PIECES = 4
VMEM = 61 * 1024 * 1024
NN = (((1,), (0,)), ((), ()))
NT = (((1,), (1,)), ((), ()))


def split(x):
    hi = x.astype(jnp.bfloat16)
    lo = (x - hi.astype(jnp.float32)).astype(jnp.bfloat16)
    return hi, lo


def dot(a, b, dims):
    return lax.dot_general(a, b, dims, preferred_element_type=jnp.float32)


def dot3(a_both, b, dims):
    rows = a_both.shape[0] // 2
    b_hi, b_lo = b
    both = dot(a_both, b_hi, dims)
    return both[:rows] + both[rows:] + dot(a_both[:rows], b_lo, dims)


def block_of(size, most):
    block = size
    while block > most and block % 2 == 0:
        block //= 2
    return block


def light():
    return pl.CostEstimate(flops=1, bytes_accessed=1, transcendentals=0)


def pass_over(factor, chunk, columns, fitted=None, parts=None, gaps=None, stored=None, which=None, before=None, after=(), pieces=PIECES, most=2048):
    aux = factor.shape[1]
    block = block_of(columns, most)
    steps = columns // block
    first = chunk * steps
    out_rows = fitted.shape[0] if fitted is not None else 0
    half = out_rows // 2
    piece = half // pieces
    wide = gaps is not None
    own = extra = 0
    if wide:
        own = stored.shape[0] // which[1]
        extra = -(-own // 128) * 128
    parts = parts or []
    rows = sum(p.shape[0] for p in parts)
    after = [a for a in after if a is not None]

    def kernel(*refs):
        refs = list(refs)
        if wide:
            refs.pop(0)
        f_ref = refs.pop(0)
        if half:
            t_ref = refs.pop(0)
        xs = [refs.pop(0) for _ in parts]
        if wide:
            g_ref, s_ref = refs.pop(0), refs.pop(0)
        b_ref = refs.pop(0) if before is not None else None
        for _ in after:
            refs.pop(0)
        if half:
            keep_ref = refs.pop(0)
            send_refs = [refs.pop(0) for _ in range(pieces)]
        o_ref = refs.pop(0) if parts else None
        if half:
            both_ref = refs.pop(0)

        @pl.when(pl.program_id(0) == 0)
        def _():
            if half:
                hi, lo = split(4.0 * t_ref[...])
                both_ref[:out_rows] = hi
                both_ref[out_rows:] = lo
            if parts:
                if b_ref is None:
                    o_ref[...] = jnp.zeros_like(o_ref)
                else:
                    o_ref[...] = b_ref[...]

        factors = split(f_ref[...])
        if half:
            out = dot3(both_ref[...], factors, NT)
            keep_ref[...] = out[:half]
            for i, r in enumerate(send_refs):
                r[...] = out[half + i * piece : half + (i + 1) * piece]
        if parts:
            x = jnp.concatenate([r[...] for r in xs], axis=0) if len(xs) > 1 else xs[0][...]
            o_ref[:, :aux] += dot3(jnp.concatenate(split(x), axis=0), factors, NN)
            if wide:
                both = jnp.concatenate(split(x * g_ref[...]), axis=0)
                o_ref[:, aux : aux + own] += dot3(both, split(s_ref[...]), NT)

    in_specs = [pl.BlockSpec((block, aux), lambda k, *_: (first + k, 0))]
    args = [factor]
    if half:
        in_specs.append(pl.BlockSpec((out_rows, aux), lambda k, *_: (0, 0)))
        args.append(fitted)
    for p in parts:
        offset = first if p.shape[1] != columns else 0
        in_specs.append(pl.BlockSpec((p.shape[0], block), lambda k, *_, offset=offset: (0, offset + k)))
        args.append(p)
    if wide:
        in_specs.append(pl.BlockSpec((1, block), lambda k, *_: (0, first + k)))
        in_specs.append(pl.BlockSpec((own, block), lambda k, a: (a[0], first + k)))
        args += [gaps, stored]
    if before is not None:
        in_specs.append(pl.BlockSpec(before.shape, lambda k, *_: (0, 0)))
        args.append(before)
    for a in after:
        in_specs.append(pl.BlockSpec(memory_space=pl.ANY))
        args.append(a)
    shapes, specs = [], []
    if half:
        for height in [half] + [piece] * pieces:
            shapes.append(jax.ShapeDtypeStruct((height, columns), jnp.float32))
            specs.append(pl.BlockSpec((height, block), lambda k, *_: (0, k)))
    if parts:
        shapes.append(jax.ShapeDtypeStruct((rows, aux + extra), jnp.float32))
        specs.append(pl.BlockSpec((rows, aux + extra), lambda k, *_: (0, 0)))
    if wide:
        args = [which[0]] + args
    out = pl.pallas_call(
        kernel,
        out_shape=tuple(shapes),
        grid_spec=pltpu.PrefetchScalarGridSpec(
            num_scalar_prefetch=1 if wide else 0,
            grid=(steps,),
            in_specs=in_specs,
            out_specs=tuple(specs),
            scratch_shapes=[pltpu.VMEM((2 * out_rows, aux), jnp.bfloat16)] if half else [],
        ),
        compiler_params=pltpu.CompilerParams(vmem_limit_bytes=VMEM),
        cost_estimate=light(),
        name=("spread" if half else "") + ("fit" if parts else ""),
    )(*args)
    if half:
        out = [out[0], list(out[1 : 1 + pieces]), *out[1 + pieces :]]
    return out


def whole(refs):
    return jnp.concatenate([r[...] for r in refs], axis=0) if len(refs) > 1 else refs[0][...]


def assemble(summed, arrived, olds, old_chunks, projection, stored, gaps, chunk, swap, after=(), most=2048):
    rows = sum(a.shape[0] for a in arrived)
    columns = arrived[0].shape[1]
    total = stored.shape[0]
    block = block_of(columns, most)
    steps = columns // block
    first = chunk * steps
    half = rows // 2
    pieces = PIECES if swap else 1
    piece = rows // pieces

    def kernel(*refs):
        refs = list(refs)
        cs = [refs.pop(0) for _ in summed]
        ys = [refs.pop(0) for _ in arrived]
        xs = [refs.pop(0) for _ in olds]
        p_ref, s_ref, g_ref = refs[:3]
        o_refs, q_ref = refs[-1 - pieces : -1], refs[-1]
        arrival = whole(ys)
        if swap:
            arrival = jnp.concatenate([arrival[half:], arrival[:half]], axis=0)
        x = whole(xs)
        both = jnp.concatenate(split(p_ref[...]), axis=0)
        removed = dot3(both, split(s_ref[...]), NN)
        new = x + (whole(cs) + arrival - removed) / g_ref[...]
        for i, r in enumerate(o_refs):
            r[...] = new[i * piece : (i + 1) * piece]

        @pl.when(pl.program_id(0) == 0)
        def _():
            q_ref[...] = jnp.zeros_like(q_ref)

        q_ref[...] += jnp.sum(new * new, axis=1, keepdims=True)

    def old_spec(height, offset):
        return pl.BlockSpec((height, block), lambda k: (0, offset * steps + k))

    in_specs = [pl.BlockSpec((a.shape[0], block), lambda k: (0, k)) for a in (*summed, *arrived)]
    share = rows // len(olds)
    in_specs += [old_spec(share, c) for c in old_chunks]
    in_specs += [
        pl.BlockSpec((rows, total), lambda k: (0, 0)),
        pl.BlockSpec((total, block), lambda k: (0, first + k)),
        pl.BlockSpec((1, block), lambda k: (0, first + k)),
    ]
    in_specs += [pl.BlockSpec(memory_space=pl.ANY) for _ in after]
    *new, squares = pl.pallas_call(
        kernel,
        out_shape=(
            *[jax.ShapeDtypeStruct((piece, columns), jnp.float32)] * pieces,
            jax.ShapeDtypeStruct((rows, 128), jnp.float32),
        ),
        grid=(steps,),
        in_specs=in_specs,
        out_specs=(
            *[pl.BlockSpec((piece, block), lambda k: (0, k))] * pieces,
            pl.BlockSpec((rows, 128), lambda k: (0, 0)),
        ),
        compiler_params=pltpu.CompilerParams(vmem_limit_bytes=VMEM),
        cost_estimate=light(),
        name="assemble",
    )(*summed, *arrived, *olds, projection, stored, gaps, *after)
    return new, squares


def swap_with(value, axis, size, distance):
    return lax.ppermute(value, axis, [(i, i ^ distance) for i in range(size)])


def small(kernel, shapes, *args, name="small", scalar=None, after=()):
    out = tuple(jax.ShapeDtypeStruct(x, jnp.float32) for x in shapes)
    specs = [pl.BlockSpec(memory_space=pltpu.VMEM)] * len(args)
    if scalar is not None:
        specs = [pl.BlockSpec(memory_space=pltpu.SMEM)] + specs
        args = (scalar, *args)
    used = len(args)

    def body(*refs):
        kernel(*refs[:used], *refs[used + len(after) :])

    specs += [pl.BlockSpec(memory_space=pl.ANY)] * len(after)
    args = (*args, *after)
    return pl.pallas_call(
        body,
        out_shape=out,
        in_specs=specs,
        out_specs=tuple(pl.BlockSpec(memory_space=pltpu.VMEM) for _ in out),
        compiler_params=pltpu.CompilerParams(vmem_limit_bytes=VMEM),
        cost_estimate=light(),
        name=name,
    )(*args)


def total_of(*values, after=()):
    def kernel(*refs):
        acc = refs[0][...]
        for r in refs[1:-1]:
            acc = acc + r[...]
        refs[-1][...] = acc

    return small(kernel, [values[0].shape], *values, name="total", after=after)[0]


def joined(keep, near, parts, after=(), most=4096):
    rows, columns = keep.shape
    block = block_of(columns, most)
    each = near[0].shape[0]
    height = rows // parts

    def kernel(k_ref, *refs):
        ins, outs = refs[: len(near)], refs[len(near) + len(after) :]
        for i, r in enumerate(ins):
            at = i * each
            outs[at // height][at % height : at % height + each] = k_ref[at : at + each] + r[...]

    return pl.pallas_call(
        kernel,
        out_shape=tuple([jax.ShapeDtypeStruct((height, columns), jnp.float32)] * parts),
        grid=(columns // block,),
        in_specs=[pl.BlockSpec((rows, block), lambda k: (0, k))]
        + [pl.BlockSpec((each, block), lambda k: (0, k))] * len(near)
        + [pl.BlockSpec(memory_space=pl.ANY)] * len(after),
        out_specs=tuple([pl.BlockSpec((height, block), lambda k: (0, k))] * parts),
        compiler_params=pltpu.CompilerParams(vmem_limit_bytes=VMEM),
        cost_estimate=light(),
        name="joined",
    )(keep, *near, *after)


def pair_sum(value, size, between=(None, None), last=None, after=()):
    rows, columns = value.shape
    block = rows // 4
    me = jnp.reshape(lax.axis_index("pair") % 4, (1,)).astype(jnp.int32)

    def cut(m_ref, v_ref, *out):
        for d, o in enumerate(out):
            o[...] = v_ref[pl.ds(pl.multiple_of((m_ref[0] ^ d) * block, 8), block), :]

    def gather(m_ref, *refs):
        for d, r in enumerate(refs[:-1]):
            refs[-1][pl.ds(pl.multiple_of((m_ref[0] ^ d) * block, 8), block), :] = r[...]

    mine, *rest = small(cut, [(block, columns)] * 4, value, scalar=me, name="cut", after=after)
    others = [swap_with(r, "pair", size, d) for d, r in enumerate(rest, 1)]
    after = [between[0]([mine])] if between[0] else []
    total = total_of(mine, *others, after=after)
    distance = 4
    while distance < size:
        other = swap_with(total, "pair", size, distance)
        after = [between[1]([total])] if between[1] and distance == 4 else []
        total = total_of(total, other, after=after)
        distance *= 2
    every = [total] + [swap_with(total, "pair", size, d) for d in (1, 2, 3)]
    after = [last([total])] if last else []
    return small(gather, [(rows, columns)], *every, scalar=me, name="gather", after=after)[0]


def small_sum(value, size):
    if size & (size - 1):
        return lax.psum(value, "pair")
    distance = 1
    while distance < size:
        value = value + swap_with(value, "pair", size, distance)
        distance *= 2
    return value


def on_device(n_pair, n_aux, factor, trials, stored, energy_gaps):
    local, aux = factor.shape
    total = stored.shape[0]
    pairs = local * n_pair
    owned = trials.shape[0]
    own_s = total // n_aux
    me = lax.axis_index("aux")
    which = (jnp.reshape(me, (1,)).astype(jnp.int32), n_aux)
    gaps = energy_gaps[None, :]
    chunks = 2
    h = owned // 2
    two = 2 * h
    kc = local // chunks
    aux_swap = functools.partial(swap_with, axis="aux", size=n_aux)
    over = functools.partial(pass_over, factor)
    wide = dict(gaps=gaps, stored=stored, which=which)

    def project(fitted):
        def part(m_ref, f_ref, w_ref, keep_ref, send_ref):
            f = jnp.concatenate(split(4.0 * f_ref[:, :aux]), axis=0)
            own = f_ref[:, aux:]
            shape = (own.shape[1], total)
            row = lax.broadcasted_iota(jnp.int32, shape, 0)
            column = lax.broadcasted_iota(jnp.int32, shape, 1)
            here = (column == row + m_ref[0] * own_s) & (row < own_s)
            here = jnp.where(here, 1.0, 0.0).astype(jnp.bfloat16)
            placed = dot(jnp.concatenate(split(own), axis=0), here, NN)
            rows = own.shape[0]
            out = dot3(f, split(w_ref[...]), NT) + placed[:rows] + placed[rows:]
            keep_ref[...] = out[:two]
            send_ref[...] = out[two:]

        def both(k_ref, t_ref, o_ref):
            o_ref[:h] = k_ref[:h] + t_ref[h:]
            o_ref[h:] = k_ref[h:] + t_ref[:h]

        keep, send = small(part, [(two, total)] * 2, fitted, crossed, scalar=which[0], name="project")
        first_part = keep
        keep = total_of(keep, aux_swap(send, distance=1))
        part_sum = small(both, [(two, total)], keep, aux_swap(keep, distance=2), name="both")[0]
        return first_part, part_sum

    everyone = []
    for g in range(2):
        own = trials[g * h : (g + 1) * h]
        everyone.append([own, aux_swap(own, distance=2)])

    def near_too(parts, token):
        parts = lax.optimization_barrier((*parts, token))[:2]
        return [*parts, *(aux_swap(p, distance=1) for p in parts)]

    (crossed,) = over(0, local, parts=[stored])
    everyone[0] = near_too(everyone[0], crossed)
    held = [None]

    def first_fit(c):
        def run(after):
            held.extend(over(c, kc, parts=everyone[0], before=held[-1], after=after, **wide))
            return held[-1]

        return run

    begins = []

    def first_way(after):
        begins.append(pair_sum(held[-1], n_pair, after=after))
        everyone[1] = near_too(everyone[1], begins[0])
        begins.append(over(0, kc, fitted=begins[0], parts=everyone[1], **wide))
        return begins[1][2]

    crossed = pair_sum(crossed, n_pair, (first_fit(0), first_fit(1)), first_way)
    one = begins[0]

    def summed(keep, send, after):
        (keep,) = joined(keep, [aux_swap(x, distance=1) for x in send], 1, after)
        return [keep], [aux_swap(keep, distance=2)]

    def new_vectors(g, c, pair, projection, token):
        new, square = assemble(
            *pair, everyone[g][:2], (c, c), projection, stored, gaps, c, True, after=token
        )
        return new + [aux_swap(x, distance=1) for x in new], square[:h]

    begun, first = project(one)
    projected = [[None, None], [None, None]]
    projected[0][0] = first[:h]
    keep, send, partial = begins[1]
    sent = [[summed(keep, send, [first])], []]
    for c in range(1, chunks):
        keep, send, partial = over(
            c, kc, fitted=one, parts=everyone[1], before=partial, after=[sent[0][-1][0][0]], **wide
        )
        sent[0].append(summed(keep, send, []))
    two_sum = pair_sum(partial, n_pair)
    current = [[], []]
    squares = [0.0, 0.0]
    begun, second = project(two_sum)
    projected[0][1] = second[:h]

    partial, token = None, [two_sum, sent[0][-1][0][0]]
    for c in range(chunks):
        x, square = new_vectors(0, c, sent[0][c], first, token)
        current[0].append(x)
        squares[0] = squares[0] + square
        keep, send, partial = over(c, kc, fitted=two_sum, parts=x, before=partial, after=[begun], **wide)
        sent[1].append(summed(keep, send, [second]))
        token = [sent[1][-1][0][0]]
    one = pair_sum(partial, n_pair)
    begun, aux_sum = project(one)
    first = aux_sum[:h]
    projected[1][0] = first

    def last_sum(keep, send, after, split_in=1):
        near = [aux_swap(x, distance=1) for x in send]
        out = joined(keep, near, 2 * split_in, after)
        return out[:split_in], [aux_swap(x, distance=2) for x in out[split_in:]]

    partial, last = None, [[], []]
    for c in range(chunks):
        x, square = new_vectors(1, c, sent[1][c], second, token)
        current[1].append(x)
        squares[1] = squares[1] + square
        if c == 0:
            keep, send, partial = over(c, kc, fitted=one, parts=x, before=partial, after=[begun], **wide)
            last[0].append(last_sum(keep, send, [aux_sum]))
            keep, send = over(c + 1, kc, fitted=one, after=[last[0][-1][0][0]])
            last[0].append(last_sum(keep, send, []))
            token = [last[0][-1][0][0]]
        else:
            (partial,) = over(c, kc, parts=x, before=partial, **wide)
    ends = [[], []]
    norms = [0.0, 0.0]

    def finish(g, c, projection, token):
        new, square = assemble(
            *last[g][c],
            current[g][c][: PIECES // 2],
            (0,) * (PIECES // 2),
            projection,
            stored,
            gaps,
            c,
            False,
            after=token,
        )
        ends[g].append(new[0])
        norms[g] = norms[g] + square
        return new[0]

    two_sum = pair_sum(
        partial,
        n_pair,
        (lambda after: finish(0, 0, first, after), lambda after: finish(0, 1, first, after)),
    )
    begun, aux_sum = project(two_sum)
    second = aux_sum[:h]
    projected[1][1] = second
    token = [begun]
    for c in range(chunks):
        keep, send = over(c, kc, fitted=two_sum, after=token)
        last[1].append(last_sum(keep, send, [aux_sum]))
        token = [last[1][-1][0][0]]
    token = []
    for c in range(chunks):
        token = [finish(1, c, second, token)]

    sums = jnp.concatenate([jnp.concatenate(squares, 0), jnp.concatenate(norms, 0)], axis=1)
    sums = small_sum(sums, n_pair)
    norm = jnp.sqrt(sums[:, :1] / pairs + 1e-06)
    scale = norm * jnp.sqrt(sums[:, 128:129] / (norm * norm) / pairs + 1e-06)
    out = jnp.concatenate([jnp.concatenate(e, axis=1) for e in ends], axis=0) / scale
    first_p = jnp.concatenate(projected[0], axis=0)
    second_p = jnp.concatenate(projected[1], axis=0) / norm
    return out, jnp.stack([first_p.T, second_p.T])


def solution(mesh):
    in_specs = (P("pair", "aux"), P("aux", "pair"), P(None, "pair"), P("pair"))
    out_specs = (P("aux", "pair"), P(None, None, "aux"))
    body = functools.partial(on_device, mesh.shape["pair"], mesh.shape["aux"])
    return jax.shard_map(body, mesh=mesh, in_specs=in_specs, out_specs=out_specs, check_vma=False)
```

```python
import functools

import jax
import jax.numpy as jnp
from jax import lax
from jax.experimental import pallas as pl
from jax.experimental.pallas import tpu as pltpu
from jax.sharding import PartitionSpec as P

ROUNDS = 2
PIECES = 4
VMEM = 56 * 1024 * 1024
NN = (((1,), (0,)), ((), ()))
NT = (((1,), (1,)), ((), ()))


def split(x):
    hi = x.astype(jnp.bfloat16)
    lo = (x - hi.astype(jnp.float32)).astype(jnp.bfloat16)
    return hi, lo


def dot(a, b, dims):
    return lax.dot_general(a, b, dims, preferred_element_type=jnp.float32)


def dot3(a_both, b, dims):
    rows = a_both.shape[0] // 2
    b_hi, b_lo = b
    both = dot(a_both, b_hi, dims)
    return both[:rows] + both[rows:] + dot(a_both[:rows], b_lo, dims)


def block_of(size, most):
    block = size
    while block > most and block % 2 == 0:
        block //= 2
    return block


def light():
    return pl.CostEstimate(flops=1, bytes_accessed=1, transcendentals=0)


def pass_over(factor, chunk, columns, fitted=None, parts=None, gaps=None, stored=None, which=None, before=None, after=(), pieces=PIECES, most=2048):
    aux = factor.shape[1]
    block = block_of(columns, most)
    steps = columns // block
    first = chunk * steps
    out_rows = fitted.shape[0] if fitted is not None else 0
    half = out_rows // 2
    piece = half // pieces
    wide = gaps is not None
    own = extra = 0
    if wide:
        own = stored.shape[0] // which[1]
        extra = -(-own // 128) * 128
    parts = parts or []
    rows = sum(p.shape[0] for p in parts)
    after = [a for a in after if a is not None]

    def kernel(*refs):
        refs = list(refs)
        if wide:
            refs.pop(0)
        f_ref = refs.pop(0)
        if half:
            t_ref = refs.pop(0)
        xs = [refs.pop(0) for _ in parts]
        if wide:
            g_ref, s_ref = refs.pop(0), refs.pop(0)
        b_ref = refs.pop(0) if before is not None else None
        for _ in after:
            refs.pop(0)
        if half:
            keep_ref = refs.pop(0)
            send_refs = [refs.pop(0) for _ in range(pieces)]
        o_ref = refs.pop(0) if parts else None
        if half:
            both_ref = refs.pop(0)

        @pl.when(pl.program_id(0) == 0)
        def _():
            if half:
                hi, lo = split(4.0 * t_ref[...])
                both_ref[:out_rows] = hi
                both_ref[out_rows:] = lo
            if parts:
                if b_ref is None:
                    o_ref[...] = jnp.zeros_like(o_ref)
                else:
                    o_ref[...] = b_ref[...]

        factors = split(f_ref[...])
        if half:
            out = dot3(both_ref[...], factors, NT)
            keep_ref[...] = out[:half]
            for i, r in enumerate(send_refs):
                r[...] = out[half + i * piece : half + (i + 1) * piece]
        if parts:
            x = jnp.concatenate([r[...] for r in xs], axis=0) if len(xs) > 1 else xs[0][...]
            o_ref[:, :aux] += dot3(jnp.concatenate(split(x), axis=0), factors, NN)
            if wide:
                both = jnp.concatenate(split(x * g_ref[...]), axis=0)
                o_ref[:, aux : aux + own] += dot3(both, split(s_ref[...]), NT)

    in_specs = [pl.BlockSpec((block, aux), lambda k, *_: (first + k, 0))]
    args = [factor]
    if half:
        in_specs.append(pl.BlockSpec((out_rows, aux), lambda k, *_: (0, 0)))
        args.append(fitted)
    for p in parts:
        offset = first if p.shape[1] != columns else 0
        in_specs.append(pl.BlockSpec((p.shape[0], block), lambda k, *_, offset=offset: (0, offset + k)))
        args.append(p)
    if wide:
        in_specs.append(pl.BlockSpec((1, block), lambda k, *_: (0, first + k)))
        in_specs.append(pl.BlockSpec((own, block), lambda k, a: (a[0], first + k)))
        args += [gaps, stored]
    if before is not None:
        in_specs.append(pl.BlockSpec(before.shape, lambda k, *_: (0, 0)))
        args.append(before)
    for a in after:
        in_specs.append(pl.BlockSpec(memory_space=pl.ANY))
        args.append(a)
    shapes, specs = [], []
    if half:
        for height in [half] + [piece] * pieces:
            shapes.append(jax.ShapeDtypeStruct((height, columns), jnp.float32))
            specs.append(pl.BlockSpec((height, block), lambda k, *_: (0, k)))
    if parts:
        shapes.append(jax.ShapeDtypeStruct((rows, aux + extra), jnp.float32))
        specs.append(pl.BlockSpec((rows, aux + extra), lambda k, *_: (0, 0)))
    if wide:
        args = [which[0]] + args
    out = pl.pallas_call(
        kernel,
        out_shape=tuple(shapes),
        grid_spec=pltpu.PrefetchScalarGridSpec(
            num_scalar_prefetch=1 if wide else 0,
            grid=(steps,),
            in_specs=in_specs,
            out_specs=tuple(specs),
            scratch_shapes=[pltpu.VMEM((2 * out_rows, aux), jnp.bfloat16)] if half else [],
        ),
        compiler_params=pltpu.CompilerParams(vmem_limit_bytes=VMEM),
        cost_estimate=light(),
        name=("spread" if half else "") + ("fit" if parts else ""),
    )(*args)
    if half:
        out = [out[0], list(out[1 : 1 + pieces]), *out[1 + pieces :]]
    return out


def whole(refs):
    return jnp.concatenate([r[...] for r in refs], axis=0) if len(refs) > 1 else refs[0][...]


def assemble(summed, arrived, olds, old_chunks, projection, stored, gaps, chunk, swap, after=(), most=2048):
    rows = sum(a.shape[0] for a in arrived)
    columns = arrived[0].shape[1]
    total = stored.shape[0]
    block = block_of(columns, most)
    steps = columns // block
    first = chunk * steps
    half = rows // 2
    pieces = PIECES if swap else 1
    piece = rows // pieces

    def kernel(*refs):
        refs = list(refs)
        cs = [refs.pop(0) for _ in summed]
        ys = [refs.pop(0) for _ in arrived]
        xs = [refs.pop(0) for _ in olds]
        p_ref, s_ref, g_ref = refs[:3]
        o_refs, q_ref = refs[-1 - pieces : -1], refs[-1]
        arrival = whole(ys)
        if swap:
            arrival = jnp.concatenate([arrival[half:], arrival[:half]], axis=0)
        x = whole(xs)
        both = jnp.concatenate(split(p_ref[...]), axis=0)
        removed = dot3(both, split(s_ref[...]), NN)
        new = x + (whole(cs) + arrival - removed) / g_ref[...]
        for i, r in enumerate(o_refs):
            r[...] = new[i * piece : (i + 1) * piece]

        @pl.when(pl.program_id(0) == 0)
        def _():
            q_ref[...] = jnp.zeros_like(q_ref)

        q_ref[...] += jnp.sum(new * new, axis=1, keepdims=True)

    def old_spec(height, offset):
        return pl.BlockSpec((height, block), lambda k: (0, offset * steps + k))

    in_specs = [pl.BlockSpec((a.shape[0], block), lambda k: (0, k)) for a in (*summed, *arrived)]
    share = rows // len(olds)
    in_specs += [old_spec(share, c) for c in old_chunks]
    in_specs += [
        pl.BlockSpec((rows, total), lambda k: (0, 0)),
        pl.BlockSpec((total, block), lambda k: (0, first + k)),
        pl.BlockSpec((1, block), lambda k: (0, first + k)),
    ]
    in_specs += [pl.BlockSpec(memory_space=pl.ANY) for _ in after]
    *new, squares = pl.pallas_call(
        kernel,
        out_shape=(
            *[jax.ShapeDtypeStruct((piece, columns), jnp.float32)] * pieces,
            jax.ShapeDtypeStruct((rows, 128), jnp.float32),
        ),
        grid=(steps,),
        in_specs=in_specs,
        out_specs=(
            *[pl.BlockSpec((piece, block), lambda k: (0, k))] * pieces,
            pl.BlockSpec((rows, 128), lambda k: (0, 0)),
        ),
        compiler_params=pltpu.CompilerParams(vmem_limit_bytes=VMEM),
        cost_estimate=light(),
        name="assemble",
    )(*summed, *arrived, *olds, projection, stored, gaps, *after)
    return new, squares


def swap_with(value, axis, size, distance):
    return lax.ppermute(value, axis, [(i, i ^ distance) for i in range(size)])


def small(kernel, shapes, *args, name="small", scalar=None, after=()):
    out = tuple(jax.ShapeDtypeStruct(x, jnp.float32) for x in shapes)
    specs = [pl.BlockSpec(memory_space=pltpu.VMEM)] * len(args)
    if scalar is not None:
        specs = [pl.BlockSpec(memory_space=pltpu.SMEM)] + specs
        args = (scalar, *args)
    used = len(args)

    def body(*refs):
        kernel(*refs[:used], *refs[used + len(after) :])

    specs += [pl.BlockSpec(memory_space=pl.ANY)] * len(after)
    args = (*args, *after)
    return pl.pallas_call(
        body,
        out_shape=out,
        in_specs=specs,
        out_specs=tuple(pl.BlockSpec(memory_space=pltpu.VMEM) for _ in out),
        compiler_params=pltpu.CompilerParams(vmem_limit_bytes=VMEM // 2),
        cost_estimate=light(),
        name=name,
    )(*args)


def total_of(*values, after=()):
    def kernel(*refs):
        acc = refs[0][...]
        for r in refs[1:-1]:
            acc = acc + r[...]
        refs[-1][...] = acc

    return small(kernel, [values[0].shape], *values, name="total", after=after)[0]


def joined(keep, near, parts, after=(), most=4096):
    rows, columns = keep.shape
    block = block_of(columns, most)
    each = near[0].shape[0]
    height = rows // parts

    def kernel(k_ref, *refs):
        ins, outs = refs[: len(near)], refs[len(near) + len(after) :]
        for i, r in enumerate(ins):
            at = i * each
            outs[at // height][at % height : at % height + each] = k_ref[at : at + each] + r[...]

    return pl.pallas_call(
        kernel,
        out_shape=tuple([jax.ShapeDtypeStruct((height, columns), jnp.float32)] * parts),
        grid=(columns // block,),
        in_specs=[pl.BlockSpec((rows, block), lambda k: (0, k))]
        + [pl.BlockSpec((each, block), lambda k: (0, k))] * len(near)
        + [pl.BlockSpec(memory_space=pl.ANY)] * len(after),
        out_specs=tuple([pl.BlockSpec((height, block), lambda k: (0, k))] * parts),
        compiler_params=pltpu.CompilerParams(vmem_limit_bytes=VMEM),
        cost_estimate=light(),
        name="joined",
    )(keep, *near, *after)


def pair_sum(value, size, between=(None, None), last=None, after=()):
    rows, columns = value.shape
    block = rows // 4
    me = jnp.reshape(lax.axis_index("pair") % 4, (1,)).astype(jnp.int32)

    def cut(m_ref, v_ref, *out):
        for d, o in enumerate(out):
            o[...] = v_ref[pl.ds(pl.multiple_of((m_ref[0] ^ d) * block, 8), block), :]

    def gather(m_ref, *refs):
        for d, r in enumerate(refs[:-1]):
            refs[-1][pl.ds(pl.multiple_of((m_ref[0] ^ d) * block, 8), block), :] = r[...]

    mine, *rest = small(cut, [(block, columns)] * 4, value, scalar=me, name="cut", after=after)
    others = [swap_with(r, "pair", size, d) for d, r in enumerate(rest, 1)]
    after = [between[0]([mine])] if between[0] else []
    total = total_of(mine, *others, after=after)
    distance = 4
    while distance < size:
        other = swap_with(total, "pair", size, distance)
        after = [between[1]([total])] if between[1] and distance == 4 else []
        total = total_of(total, other, after=after)
        distance *= 2
    every = [total] + [swap_with(total, "pair", size, d) for d in (1, 2, 3)]
    after = [last([total])] if last else []
    return small(gather, [(rows, columns)], *every, scalar=me, name="gather", after=after)[0]


def small_sum(value, size):
    if size & (size - 1):
        return lax.psum(value, "pair")
    distance = 1
    while distance < size:
        value = value + swap_with(value, "pair", size, distance)
        distance *= 2
    return value


def on_device(n_pair, n_aux, factor, trials, stored, energy_gaps):
    local, aux = factor.shape
    total = stored.shape[0]
    pairs = local * n_pair
    owned = trials.shape[0]
    own_s = total // n_aux
    me = lax.axis_index("aux")
    which = (jnp.reshape(me, (1,)).astype(jnp.int32), n_aux)
    gaps = energy_gaps[None, :]
    chunks = 2
    h = owned // 2
    two = 2 * h
    kc = local // chunks
    aux_swap = functools.partial(swap_with, axis="aux", size=n_aux)
    over = functools.partial(pass_over, factor)
    wide = dict(gaps=gaps, stored=stored, which=which)

    def project(fitted):
        def part(m_ref, f_ref, w_ref, keep_ref, send_ref):
            f = jnp.concatenate(split(4.0 * f_ref[:, :aux]), axis=0)
            own = f_ref[:, aux:]
            shape = (own.shape[1], total)
            row = lax.broadcasted_iota(jnp.int32, shape, 0)
            column = lax.broadcasted_iota(jnp.int32, shape, 1)
            here = (column == row + m_ref[0] * own_s) & (row < own_s)
            here = jnp.where(here, 1.0, 0.0).astype(jnp.bfloat16)
            placed = dot(jnp.concatenate(split(own), axis=0), here, NN)
            rows = own.shape[0]
            out = dot3(f, split(w_ref[...]), NT) + placed[:rows] + placed[rows:]
            keep_ref[...] = out[:two]
            send_ref[...] = out[two:]

        def both(k_ref, t_ref, o_ref):
            o_ref[:h] = k_ref[:h] + t_ref[h:]
            o_ref[h:] = k_ref[h:] + t_ref[:h]

        keep, send = small(part, [(two, total)] * 2, fitted, crossed, scalar=which[0], name="project")
        first_part = keep
        keep = total_of(keep, aux_swap(send, distance=1))
        part_sum = small(both, [(two, total)], keep, aux_swap(keep, distance=2), name="both")[0]
        return first_part, part_sum

    everyone = []
    for g in range(2):
        own = trials[g * h : (g + 1) * h]
        everyone.append([own, aux_swap(own, distance=2)])

    def near_too(parts, token):
        parts = lax.optimization_barrier((*parts, token))[:2]
        return [*parts, *(aux_swap(p, distance=1) for p in parts)]

    (crossed,) = over(0, local, parts=[stored])
    everyone[0] = near_too(everyone[0], crossed)
    held = [None]

    def first_fit(c):
        def run(after):
            held.extend(over(c, kc, parts=everyone[0], before=held[-1], after=after, **wide))
            return held[-1]

        return run

    begins = []

    def first_way(after):
        begins.append(pair_sum(held[-1], n_pair, after=after))
        everyone[1] = near_too(everyone[1], begins[0])
        begins.append(over(0, kc, fitted=begins[0], parts=everyone[1], **wide))
        return begins[1][2]

    crossed = pair_sum(crossed, n_pair, (first_fit(0), first_fit(1)), first_way)
    one = begins[0]

    def summed(keep, send, after):
        (keep,) = joined(keep, [aux_swap(x, distance=1) for x in send], 1, after)
        return [keep], [aux_swap(keep, distance=2)]

    def new_vectors(g, c, projection, token):
        new, square = assemble(
            *sent[g][c], everyone[g][:2], (c, c), projection, stored, gaps, c, True, after=token
        )
        current[g].append(new + [aux_swap(x, distance=1) for x in new])
        squares[g] = squares[g] + square[:h]
        return new[0]

    begun, first = project(one)
    projected = [[None, None], [None, None]]
    projected[0][0] = first[:h]
    keep, send, partial = begins[1]
    sent = [[summed(keep, send, [first])], []]
    for c in range(1, chunks):
        keep, send, partial = over(
            c, kc, fitted=one, parts=everyone[1], before=partial, after=[sent[0][-1][0][0]], **wide
        )
        sent[0].append(summed(keep, send, []))
    two_sum = pair_sum(partial, n_pair)
    current = [[], []]
    squares = [0.0, 0.0]
    begun, second = project(two_sum)
    projected[0][1] = second[:h]

    partial, token = None, new_vectors(0, 0, first, [two_sum, sent[0][-1][0][0]])
    for c in range(chunks):
        keep, send, partial = over(
            c, kc, fitted=two_sum, parts=current[0][c], before=partial, after=[begun, token], **wide
        )
        token = partial
        if c + 1 < chunks:
            token = new_vectors(0, c + 1, first, [partial])
        sent[1].append(summed(keep, send, [second, token]))
        token = sent[1][-1][0][0]
    one = pair_sum(partial, n_pair)
    begun, aux_sum = project(one)
    first = aux_sum[:h]
    projected[1][0] = first

    def last_sum(keep, send, after, split_in=1):
        near = [aux_swap(x, distance=1) for x in send]
        out = joined(keep, near, 2 * split_in, after)
        return out[:split_in], [aux_swap(x, distance=2) for x in out[split_in:]]

    last = [[], []]
    token = new_vectors(1, 0, second, [token])
    keep, send, partial = over(0, kc, fitted=one, parts=current[1][0], after=[begun, token], **wide)
    last[0].append(last_sum(keep, send, [aux_sum]))
    for c in range(1, chunks):
        keep, send = over(c, kc, fitted=one, after=[last[0][-1][0][0]])
        last[0].append(last_sum(keep, send, []))
    for c in range(1, chunks):
        new_vectors(1, c, second, [last[0][-1][0][0]])
        (partial,) = over(c, kc, parts=current[1][c], before=partial, **wide)
    ends = [[], []]
    norms = [0.0, 0.0]

    def finish(g, c, projection, token):
        new, square = assemble(
            *last[g][c],
            current[g][c][: PIECES // 2],
            (0,) * (PIECES // 2),
            projection,
            stored,
            gaps,
            c,
            False,
            after=token,
        )
        ends[g].append(new[0])
        norms[g] = norms[g] + square
        return new[0]

    two_sum = pair_sum(
        partial,
        n_pair,
        (lambda after: finish(0, 0, first, after), lambda after: finish(0, 1, first, after)),
    )
    begun, aux_sum = project(two_sum)
    second = aux_sum[:h]
    projected[1][1] = second
    token = [begun]
    for c in range(chunks):
        keep, send = over(c, kc, fitted=two_sum, after=token, pieces=PIECES * (c + 1))
        last[1].append(last_sum(keep, send, [aux_sum], 4 if c else 1))
        token = [last[1][-1][0][0]]
    token = []
    for c in range(chunks):
        token = [finish(1, c, second, token)]

    sums = jnp.concatenate([jnp.concatenate(squares, 0), jnp.concatenate(norms, 0)], axis=1)
    sums = small_sum(sums, n_pair)
    norm = jnp.sqrt(sums[:, :1] / pairs + 1e-06)
    scale = norm * jnp.sqrt(sums[:, 128:129] / (norm * norm) / pairs + 1e-06)
    out = jnp.concatenate([jnp.concatenate(e, axis=1) for e in ends], axis=0) / scale
    first_p = jnp.concatenate(projected[0], axis=0)
    second_p = jnp.concatenate(projected[1], axis=0) / norm
    return out, jnp.stack([first_p.T, second_p.T])


def solution(mesh):
    in_specs = (P("pair", "aux"), P("aux", "pair"), P(None, "pair"), P("pair"))
    out_specs = (P("aux", "pair"), P(None, None, "aux"))
    body = functools.partial(on_device, mesh.shape["pair"], mesh.shape["aux"])
    return jax.shard_map(body, mesh=mesh, in_specs=in_specs, out_specs=out_specs, check_vma=False)
```

```python
import functools

import jax
import jax.numpy as jnp
from jax import lax
from jax.experimental import pallas as pl
from jax.experimental.pallas import tpu as pltpu
from jax.sharding import PartitionSpec as P

ROUNDS = 2
PIECES = 4
VMEM = 56 * 1024 * 1024
NN = (((1,), (0,)), ((), ()))
NT = (((1,), (1,)), ((), ()))


def split(x):
    hi = x.astype(jnp.bfloat16)
    lo = (x - hi.astype(jnp.float32)).astype(jnp.bfloat16)
    return hi, lo


def dot(a, b, dims):
    return lax.dot_general(a, b, dims, preferred_element_type=jnp.float32)


def dot3(a_both, b, dims):
    rows = a_both.shape[0] // 2
    b_hi, b_lo = b
    both = dot(a_both, b_hi, dims)
    return both[:rows] + both[rows:] + dot(a_both[:rows], b_lo, dims)


def block_of(size, most):
    block = size
    while block > most and block % 2 == 0:
        block //= 2
    return block


def light():
    return pl.CostEstimate(flops=1, bytes_accessed=1, transcendentals=0)


def pass_over(factor, chunk, columns, fitted=None, parts=None, gaps=None, stored=None, which=None, before=None, after=(), pieces=PIECES, most=2048):
    aux = factor.shape[1]
    block = block_of(columns, most)
    steps = columns // block
    first = chunk * steps
    out_rows = fitted.shape[0] if fitted is not None else 0
    half = out_rows // 2
    piece = half // pieces
    wide = gaps is not None
    own = extra = 0
    if wide:
        own = stored.shape[0] // which[1]
        extra = -(-own // 128) * 128
    parts = parts or []
    rows = sum(p.shape[0] for p in parts)
    after = [a for a in after if a is not None]

    def kernel(*refs):
        refs = list(refs)
        if wide:
            refs.pop(0)
        f_ref = refs.pop(0)
        if half:
            t_ref = refs.pop(0)
        xs = [refs.pop(0) for _ in parts]
        if wide:
            g_ref, s_ref = refs.pop(0), refs.pop(0)
        b_ref = refs.pop(0) if before is not None else None
        for _ in after:
            refs.pop(0)
        if half:
            keep_ref = refs.pop(0)
            send_refs = [refs.pop(0) for _ in range(pieces)]
        o_ref = refs.pop(0) if parts else None
        if half:
            both_ref = refs.pop(0)

        @pl.when(pl.program_id(0) == 0)
        def _():
            if half:
                hi, lo = split(4.0 * t_ref[...])
                both_ref[:out_rows] = hi
                both_ref[out_rows:] = lo
            if parts:
                if b_ref is None:
                    o_ref[...] = jnp.zeros_like(o_ref)
                else:
                    o_ref[...] = b_ref[...]

        factors = split(f_ref[...])
        if half:
            out = dot3(both_ref[...], factors, NT)
            keep_ref[...] = out[:half]
            for i, r in enumerate(send_refs):
                r[...] = out[half + i * piece : half + (i + 1) * piece]
        if parts:
            x = jnp.concatenate([r[...] for r in xs], axis=0) if len(xs) > 1 else xs[0][...]
            o_ref[:, :aux] += dot3(jnp.concatenate(split(x), axis=0), factors, NN)
            if wide:
                both = jnp.concatenate(split(x * g_ref[...]), axis=0)
                o_ref[:, aux : aux + own] += dot3(both, split(s_ref[...]), NT)

    in_specs = [pl.BlockSpec((block, aux), lambda k, *_: (first + k, 0))]
    args = [factor]
    if half:
        in_specs.append(pl.BlockSpec((out_rows, aux), lambda k, *_: (0, 0)))
        args.append(fitted)
    for p in parts:
        offset = first if p.shape[1] != columns else 0
        in_specs.append(pl.BlockSpec((p.shape[0], block), lambda k, *_, offset=offset: (0, offset + k)))
        args.append(p)
    if wide:
        in_specs.append(pl.BlockSpec((1, block), lambda k, *_: (0, first + k)))
        in_specs.append(pl.BlockSpec((own, block), lambda k, a: (a[0], first + k)))
        args += [gaps, stored]
    if before is not None:
        in_specs.append(pl.BlockSpec(before.shape, lambda k, *_: (0, 0)))
        args.append(before)
    for a in after:
        in_specs.append(pl.BlockSpec(memory_space=pl.ANY))
        args.append(a)
    shapes, specs = [], []
    if half:
        for height in [half] + [piece] * pieces:
            shapes.append(jax.ShapeDtypeStruct((height, columns), jnp.float32))
            specs.append(pl.BlockSpec((height, block), lambda k, *_: (0, k)))
    if parts:
        shapes.append(jax.ShapeDtypeStruct((rows, aux + extra), jnp.float32))
        specs.append(pl.BlockSpec((rows, aux + extra), lambda k, *_: (0, 0)))
    if wide:
        args = [which[0]] + args
    out = pl.pallas_call(
        kernel,
        out_shape=tuple(shapes),
        grid_spec=pltpu.PrefetchScalarGridSpec(
            num_scalar_prefetch=1 if wide else 0,
            grid=(steps,),
            in_specs=in_specs,
            out_specs=tuple(specs),
            scratch_shapes=[pltpu.VMEM((2 * out_rows, aux), jnp.bfloat16)] if half else [],
        ),
        compiler_params=pltpu.CompilerParams(vmem_limit_bytes=VMEM),
        cost_estimate=light(),
        name=("spread" if half else "") + ("fit" if parts else ""),
    )(*args)
    if half:
        out = [out[0], list(out[1 : 1 + pieces]), *out[1 + pieces :]]
    return out


def whole(refs):
    return jnp.concatenate([r[...] for r in refs], axis=0) if len(refs) > 1 else refs[0][...]


def assemble(summed, arrived, olds, old_chunks, projection, stored, gaps, chunk, swap, after=(), most=2048):
    rows = sum(a.shape[0] for a in arrived)
    columns = arrived[0].shape[1]
    total = stored.shape[0]
    block = block_of(columns, most)
    steps = columns // block
    first = chunk * steps
    half = rows // 2
    pieces = PIECES if swap else 1
    piece = rows // pieces

    def kernel(*refs):
        refs = list(refs)
        cs = [refs.pop(0) for _ in summed]
        ys = [refs.pop(0) for _ in arrived]
        xs = [refs.pop(0) for _ in olds]
        p_ref, s_ref, g_ref = refs[:3]
        o_refs, q_ref = refs[-1 - pieces : -1], refs[-1]
        arrival = whole(ys)
        if swap:
            arrival = jnp.concatenate([arrival[half:], arrival[:half]], axis=0)
        x = whole(xs)
        both = jnp.concatenate(split(p_ref[...]), axis=0)
        removed = dot3(both, split(s_ref[...]), NN)
        new = x + (whole(cs) + arrival - removed) / g_ref[...]
        for i, r in enumerate(o_refs):
            r[...] = new[i * piece : (i + 1) * piece]

        @pl.when(pl.program_id(0) == 0)
        def _():
            q_ref[...] = jnp.zeros_like(q_ref)

        q_ref[...] += jnp.sum(new * new, axis=1, keepdims=True)

    def old_spec(height, offset):
        return pl.BlockSpec((height, block), lambda k: (0, offset * steps + k))

    in_specs = [pl.BlockSpec((a.shape[0], block), lambda k: (0, k)) for a in (*summed, *arrived)]
    share = rows // len(olds)
    in_specs += [old_spec(share, c) for c in old_chunks]
    in_specs += [
        pl.BlockSpec((rows, total), lambda k: (0, 0)),
        pl.BlockSpec((total, block), lambda k: (0, first + k)),
        pl.BlockSpec((1, block), lambda k: (0, first + k)),
    ]
    in_specs += [pl.BlockSpec(memory_space=pl.ANY) for _ in after]
    *new, squares = pl.pallas_call(
        kernel,
        out_shape=(
            *[jax.ShapeDtypeStruct((piece, columns), jnp.float32)] * pieces,
            jax.ShapeDtypeStruct((rows, 128), jnp.float32),
        ),
        grid=(steps,),
        in_specs=in_specs,
        out_specs=(
            *[pl.BlockSpec((piece, block), lambda k: (0, k))] * pieces,
            pl.BlockSpec((rows, 128), lambda k: (0, 0)),
        ),
        compiler_params=pltpu.CompilerParams(vmem_limit_bytes=VMEM),
        cost_estimate=light(),
        name="assemble",
    )(*summed, *arrived, *olds, projection, stored, gaps, *after)
    return new, squares


def swap_with(value, axis, size, distance):
    return lax.ppermute(value, axis, [(i, i ^ distance) for i in range(size)])


def small(kernel, shapes, *args, name="small", scalar=None, after=()):
    out = tuple(jax.ShapeDtypeStruct(x, jnp.float32) for x in shapes)
    specs = [pl.BlockSpec(memory_space=pltpu.VMEM)] * len(args)
    if scalar is not None:
        specs = [pl.BlockSpec(memory_space=pltpu.SMEM)] + specs
        args = (scalar, *args)
    used = len(args)

    def body(*refs):
        kernel(*refs[:used], *refs[used + len(after) :])

    specs += [pl.BlockSpec(memory_space=pl.ANY)] * len(after)
    args = (*args, *after)
    return pl.pallas_call(
        body,
        out_shape=out,
        in_specs=specs,
        out_specs=tuple(pl.BlockSpec(memory_space=pltpu.VMEM) for _ in out),
        compiler_params=pltpu.CompilerParams(vmem_limit_bytes=VMEM // 2),
        cost_estimate=light(),
        name=name,
    )(*args)


def total_of(*values, after=()):
    def kernel(*refs):
        acc = refs[0][...]
        for r in refs[1:-1]:
            acc = acc + r[...]
        refs[-1][...] = acc

    return small(kernel, [values[0].shape], *values, name="total", after=after)[0]


def joined(keep, near, parts, after=(), most=4096):
    rows, columns = keep.shape
    block = block_of(columns, most)
    each = near[0].shape[0]
    height = rows // parts

    def kernel(k_ref, *refs):
        ins, outs = refs[: len(near)], refs[len(near) + len(after) :]
        for i, r in enumerate(ins):
            at = i * each
            outs[at // height][at % height : at % height + each] = k_ref[at : at + each] + r[...]

    return pl.pallas_call(
        kernel,
        out_shape=tuple([jax.ShapeDtypeStruct((height, columns), jnp.float32)] * parts),
        grid=(columns // block,),
        in_specs=[pl.BlockSpec((rows, block), lambda k: (0, k))]
        + [pl.BlockSpec((each, block), lambda k: (0, k))] * len(near)
        + [pl.BlockSpec(memory_space=pl.ANY)] * len(after),
        out_specs=tuple([pl.BlockSpec((height, block), lambda k: (0, k))] * parts),
        compiler_params=pltpu.CompilerParams(vmem_limit_bytes=VMEM),
        cost_estimate=light(),
        name="joined",
    )(keep, *near, *after)


def quarter_index():
    return jnp.reshape(lax.axis_index("pair") % 4, (1,)).astype(jnp.int32)


def scatter_sum(value, size, hook=None, after=()):
    rows, columns = value.shape
    block = rows // 4

    def cut(m_ref, v_ref, *out):
        for d, o in enumerate(out):
            o[...] = v_ref[pl.ds(pl.multiple_of((m_ref[0] ^ d) * block, 8), block), :]

    mine, *rest = small(cut, [(block, columns)] * 4, value, scalar=quarter_index(), name="cut", after=after)
    others = [swap_with(r, "pair", size, d) for d, r in enumerate(rest, 1)]
    return total_of(mine, *others, after=[hook([mine])] if hook else [])


def across_sum(total, size, hook=None):
    distance = 4
    while distance < size:
        other = swap_with(total, "pair", size, distance)
        total = total_of(total, other, after=[hook([total])] if hook and distance == 4 else [])
        distance *= 2
    return total


def gather_all(total, size):
    block, columns = total.shape

    def gather(m_ref, *refs):
        for d, r in enumerate(refs[:-1]):
            refs[-1][pl.ds(pl.multiple_of((m_ref[0] ^ d) * block, 8), block), :] = r[...]

    every = [total] + [swap_with(total, "pair", size, d) for d in (1, 2, 3)]
    return small(gather, [(4 * block, columns)], *every, scalar=quarter_index(), name="gather")[0]


def pair_sum(value, size, between=(None, None), after=()):
    total = scatter_sum(value, size, between[0], after)
    return gather_all(across_sum(total, size, between[1]), size)


def small_sum(value, size):
    if size & (size - 1):
        return lax.psum(value, "pair")
    distance = 1
    if size % 4 == 0:
        value = total_of(value, *(swap_with(value, "pair", size, d) for d in (1, 2, 3)))
        distance = 4
    while distance < size:
        value = total_of(value, swap_with(value, "pair", size, distance))
        distance *= 2
    return value


def on_device(n_pair, n_aux, factor, trials, stored, energy_gaps):
    local, aux = factor.shape
    total = stored.shape[0]
    pairs = local * n_pair
    owned = trials.shape[0]
    own_s = total // n_aux
    me = lax.axis_index("aux")
    which = (jnp.reshape(me, (1,)).astype(jnp.int32), n_aux)
    gaps = energy_gaps[None, :]
    chunks = 2
    h = owned // 2
    two = 2 * h
    kc = local // chunks
    aux_swap = functools.partial(swap_with, axis="aux", size=n_aux)
    over = functools.partial(pass_over, factor)
    wide = dict(gaps=gaps, stored=stored, which=which)

    def project(fitted, after=()):
        def part(m_ref, f_ref, w_ref, keep_ref, send_ref):
            f = jnp.concatenate(split(4.0 * f_ref[:, :aux]), axis=0)
            own = f_ref[:, aux:]
            shape = (own.shape[1], total)
            row = lax.broadcasted_iota(jnp.int32, shape, 0)
            column = lax.broadcasted_iota(jnp.int32, shape, 1)
            here = (column == row + m_ref[0] * own_s) & (row < own_s)
            here = jnp.where(here, 1.0, 0.0).astype(jnp.bfloat16)
            placed = dot(jnp.concatenate(split(own), axis=0), here, NN)
            rows = own.shape[0]
            out = dot3(f, split(w_ref[...]), NT) + placed[:rows] + placed[rows:]
            keep_ref[...] = out[:two]
            send_ref[...] = out[two:]

        def both(k_ref, t_ref, o_ref):
            o_ref[:h] = k_ref[:h] + t_ref[h:]
            o_ref[h:] = k_ref[h:] + t_ref[:h]

        keep, send = small(part, [(two, total)] * 2, fitted, crossed, scalar=which[0], name="project", after=after)
        first_part = keep
        keep = total_of(keep, aux_swap(send, distance=1))
        part_sum = small(both, [(two, total)], keep, aux_swap(keep, distance=2), name="both")[0]
        return first_part, part_sum

    everyone = []
    for g in range(2):
        own = trials[g * h : (g + 1) * h]
        everyone.append([own, aux_swap(own, distance=2)])

    def near_too(parts, token):
        parts = lax.optimization_barrier((*parts, token))[:2]
        return [*parts, *(aux_swap(p, distance=1) for p in parts)]

    def summed(keep, send, after):
        (keep,) = joined(keep, [aux_swap(x, distance=1) for x in send], 1, after)
        return [keep], [aux_swap(keep, distance=2)]

    def new_vectors(g, c, projection, token):
        new, square = assemble(
            *sent[g][c], everyone[g][:2], (c, c), projection, stored, gaps, c, True, after=token
        )
        current[g].append(new + [aux_swap(x, distance=1) for x in new])
        squares[g] = squares[g] + square[:h]
        return new[0]

    (crossed,) = over(0, local // 2, parts=[stored])
    everyone[0] = near_too(everyone[0], crossed)
    partial, held = None, [crossed]
    for c in range(chunks):
        (partial,) = over(c, kc, parts=everyone[0], before=partial, after=[crossed], **wide)

    def other_half(after):
        held.extend(over(1, local // 2, parts=[stored], before=crossed, after=after))
        return held[-1]

    one = pair_sum(partial, n_pair, (other_half, None))
    everyone[1] = near_too(everyone[1], one)

    projected = [[None, None], [None, None]]
    current = [[], []]
    squares = [0.0, 0.0]
    sent = [[], []]
    held = [held[-1], None]

    ways = []

    def first_way(c):
        def run(after):
            if c:
                sent[0].append(summed(*ways[0], after))
                after = [*after, sent[0][0][0][0]]
            keep, send, held[1] = over(
                c, kc, fitted=one, parts=everyone[1], before=held[1], after=after, **wide
            )
            ways.append((keep, send))
            return held[1]

        return run

    crossed = pair_sum(held[0], n_pair, (first_way(0), first_way(1)))
    two_sum = scatter_sum(held[1], n_pair)
    begun, first = project(one, [two_sum])
    projected[0][0] = first[:h]
    sent[0].append(summed(*ways[1], [first]))
    firsts = []

    def early(g, projection):
        def run(after):
            firsts.append(new_vectors(g, 0, projection, after))
            return firsts[-1]

        return run

    hook = early(0, first)
    two_sum = across_sum(two_sum, n_pair, lambda after: hook([*after, sent[0][-1][0][0]]))
    two_sum = gather_all(two_sum, n_pair)
    begun, second = project(two_sum)
    projected[0][1] = second[:h]

    partial, token = None, firsts[0]
    for c in range(chunks):
        keep, send, partial = over(
            c, kc, fitted=two_sum, parts=current[0][c], before=partial, after=[begun, token], **wide
        )
        token = partial
        if c + 1 < chunks:
            token = new_vectors(0, c + 1, first, [partial])
        sent[1].append(summed(keep, send, [second, token]))
        token = sent[1][-1][0][0]
    one = pair_sum(partial, n_pair, (None, early(1, second)))
    begun, aux_sum = project(one)
    first = aux_sum[:h]
    projected[1][0] = first

    def last_sum(keep, send, after, split_in=1):
        near = [aux_swap(x, distance=1) for x in send]
        out = joined(keep, near, 2 * split_in, after)
        return out[:split_in], [aux_swap(x, distance=2) for x in out[split_in:]]

    last = [[], []]
    keep, send, partial = over(0, kc, fitted=one, parts=current[1][0], after=[begun, token], **wide)
    last[0].append(last_sum(keep, send, [aux_sum]))
    for c in range(1, chunks):
        keep, send = over(c, kc, fitted=one, after=[last[0][-1][0][0]])
        last[0].append(last_sum(keep, send, []))
    for c in range(1, chunks):
        new_vectors(1, c, second, [last[0][-1][0][0]])
        (partial,) = over(c, kc, parts=current[1][c], before=partial, **wide)
    ends = [[], []]
    norms = [0.0, 0.0]

    def finish(g, c, projection, token):
        new, square = assemble(
            *last[g][c],
            current[g][c][: PIECES // 2],
            (0,) * (PIECES // 2),
            projection,
            stored,
            gaps,
            c,
            False,
            after=token,
        )
        ends[g].append(new[0])
        norms[g] = norms[g] + square
        return new[0]

    two_sum = pair_sum(
        partial,
        n_pair,
        (lambda after: finish(0, 0, first, after), lambda after: finish(0, 1, first, after)),
    )
    begun, aux_sum = project(two_sum)
    second = aux_sum[:h]
    projected[1][1] = second
    token = [begun]
    for c in range(chunks):
        keep, send = over(c, kc, fitted=two_sum, after=token, pieces=PIECES * (c + 1))
        last[1].append(last_sum(keep, send, [aux_sum], 4 if c else 1))
        token = [last[1][-1][0][0]]
    token = []
    for c in range(chunks):
        token = [finish(1, c, second, token)]

    sums = jnp.concatenate([jnp.concatenate(squares, 0), jnp.concatenate(norms, 0)], axis=1)
    sums = small_sum(sums, n_pair)
    norm = jnp.sqrt(sums[:, :1] / pairs + 1e-06)
    scale = norm * jnp.sqrt(sums[:, 128:129] / (norm * norm) / pairs + 1e-06)
    out = jnp.concatenate([jnp.concatenate(e, axis=1) for e in ends], axis=0) / scale
    first_p = jnp.concatenate(projected[0], axis=0)
    second_p = jnp.concatenate(projected[1], axis=0) / norm
    return out, jnp.stack([first_p.T, second_p.T])


def solution(mesh):
    in_specs = (P("pair", "aux"), P("aux", "pair"), P(None, "pair"), P("pair"))
    out_specs = (P("aux", "pair"), P(None, None, "aux"))
    body = functools.partial(on_device, mesh.shape["pair"], mesh.shape["aux"])
    return jax.shard_map(body, mesh=mesh, in_specs=in_specs, out_specs=out_specs, check_vma=False)
```

```python
import functools

import jax
import jax.numpy as jnp
from jax import lax
from jax.experimental import pallas as pl
from jax.experimental.pallas import tpu as pltpu
from jax.sharding import PartitionSpec as P

ROUNDS = 2
PIECES = 4
VMEM = 56 * 1024 * 1024
NN = (((1,), (0,)), ((), ()))
NT = (((1,), (1,)), ((), ()))


def split(x):
    hi = x.astype(jnp.bfloat16)
    lo = (x - hi.astype(jnp.float32)).astype(jnp.bfloat16)
    return hi, lo


def dot(a, b, dims):
    return lax.dot_general(a, b, dims, preferred_element_type=jnp.float32)


def dot3(a_both, b, dims):
    rows = a_both.shape[0] // 2
    b_hi, b_lo = b
    both = dot(a_both, b_hi, dims)
    return both[:rows] + both[rows:] + dot(a_both[:rows], b_lo, dims)


def block_of(size, most):
    block = size
    while block > most and block % 2 == 0:
        block //= 2
    return block


def light():
    return pl.CostEstimate(flops=1, bytes_accessed=1, transcendentals=0)


def pass_over(factor, chunk, columns, fitted=None, parts=None, gaps=None, stored=None, which=None, before=None, after=(), pieces=PIECES, most=2048):
    aux = factor.shape[1]
    block = block_of(columns, most)
    steps = columns // block
    first = chunk * steps
    out_rows = fitted.shape[0] if fitted is not None else 0
    half = out_rows // 2
    piece = half // pieces
    wide = gaps is not None
    own = extra = 0
    if wide:
        own = stored.shape[0] // which[1]
        extra = -(-own // 128) * 128
    parts = parts or []
    rows = sum(p.shape[0] for p in parts)
    after = [a for a in after if a is not None]

    def kernel(*refs):
        refs = list(refs)
        if wide:
            refs.pop(0)
        f_ref = refs.pop(0)
        if half:
            t_ref = refs.pop(0)
        xs = [refs.pop(0) for _ in parts]
        if wide:
            g_ref, s_ref = refs.pop(0), refs.pop(0)
        b_ref = refs.pop(0) if before is not None else None
        for _ in after:
            refs.pop(0)
        if half:
            keep_ref = refs.pop(0)
            send_refs = [refs.pop(0) for _ in range(pieces)]
        o_ref = refs.pop(0) if parts else None
        if half:
            both_ref = refs.pop(0)

        @pl.when(pl.program_id(0) == 0)
        def _():
            if half:
                hi, lo = split(4.0 * t_ref[...])
                both_ref[:out_rows] = hi
                both_ref[out_rows:] = lo
            if parts:
                if b_ref is None:
                    o_ref[...] = jnp.zeros_like(o_ref)
                else:
                    o_ref[...] = b_ref[...]

        factors = split(f_ref[...])
        if half:
            out = dot3(both_ref[...], factors, NT)
            keep_ref[...] = out[:half]
            for i, r in enumerate(send_refs):
                r[...] = out[half + i * piece : half + (i + 1) * piece]
        if parts:
            x = jnp.concatenate([r[...] for r in xs], axis=0) if len(xs) > 1 else xs[0][...]
            o_ref[:, :aux] += dot3(jnp.concatenate(split(x), axis=0), factors, NN)
            if wide:
                both = jnp.concatenate(split(x * g_ref[...]), axis=0)
                o_ref[:, aux : aux + own] += dot3(both, split(s_ref[...]), NT)

    in_specs = [pl.BlockSpec((block, aux), lambda k, *_: (first + k, 0))]
    args = [factor]
    if half:
        in_specs.append(pl.BlockSpec((out_rows, aux), lambda k, *_: (0, 0)))
        args.append(fitted)
    for p in parts:
        offset = first if p.shape[1] != columns else 0
        in_specs.append(pl.BlockSpec((p.shape[0], block), lambda k, *_, offset=offset: (0, offset + k)))
        args.append(p)
    if wide:
        in_specs.append(pl.BlockSpec((1, block), lambda k, *_: (0, first + k)))
        in_specs.append(pl.BlockSpec((own, block), lambda k, a: (a[0], first + k)))
        args += [gaps, stored]
    if before is not None:
        in_specs.append(pl.BlockSpec(before.shape, lambda k, *_: (0, 0)))
        args.append(before)
    for a in after:
        in_specs.append(pl.BlockSpec(memory_space=pl.ANY))
        args.append(a)
    shapes, specs = [], []
    if half:
        for height in [half] + [piece] * pieces:
            shapes.append(jax.ShapeDtypeStruct((height, columns), jnp.float32))
            specs.append(pl.BlockSpec((height, block), lambda k, *_: (0, k)))
    if parts:
        shapes.append(jax.ShapeDtypeStruct((rows, aux + extra), jnp.float32))
        specs.append(pl.BlockSpec((rows, aux + extra), lambda k, *_: (0, 0)))
    if wide:
        args = [which[0]] + args
    out = pl.pallas_call(
        kernel,
        out_shape=tuple(shapes),
        grid_spec=pltpu.PrefetchScalarGridSpec(
            num_scalar_prefetch=1 if wide else 0,
            grid=(steps,),
            in_specs=in_specs,
            out_specs=tuple(specs),
            scratch_shapes=[pltpu.VMEM((2 * out_rows, aux), jnp.bfloat16)] if half else [],
        ),
        compiler_params=pltpu.CompilerParams(vmem_limit_bytes=VMEM),
        cost_estimate=light(),
        name=("spread" if half else "") + ("fit" if parts else ""),
    )(*args)
    if half:
        out = [out[0], list(out[1 : 1 + pieces]), *out[1 + pieces :]]
    return out


def whole(refs):
    return jnp.concatenate([r[...] for r in refs], axis=0) if len(refs) > 1 else refs[0][...]


def assemble(summed, arrived, olds, old_chunks, projection, stored, gaps, chunk, swap, after=(), most=2048):
    rows = sum(a.shape[0] for a in arrived)
    columns = arrived[0].shape[1]
    total = stored.shape[0]
    block = block_of(columns, most)
    steps = columns // block
    first = chunk * steps
    half = rows // 2
    pieces = PIECES if swap else 1
    piece = rows // pieces

    def kernel(*refs):
        refs = list(refs)
        cs = [refs.pop(0) for _ in summed]
        ys = [refs.pop(0) for _ in arrived]
        xs = [refs.pop(0) for _ in olds]
        p_ref, s_ref, g_ref = refs[:3]
        o_refs, q_ref = refs[-1 - pieces : -1], refs[-1]
        arrival = whole(ys)
        if swap:
            arrival = jnp.concatenate([arrival[half:], arrival[:half]], axis=0)
        x = whole(xs)
        both = jnp.concatenate(split(p_ref[...]), axis=0)
        removed = dot3(both, split(s_ref[...]), NN)
        new = x + (whole(cs) + arrival - removed) / g_ref[...]
        for i, r in enumerate(o_refs):
            r[...] = new[i * piece : (i + 1) * piece]

        @pl.when(pl.program_id(0) == 0)
        def _():
            q_ref[...] = jnp.zeros_like(q_ref)

        q_ref[...] += jnp.sum(new * new, axis=1, keepdims=True)

    def old_spec(height, offset):
        return pl.BlockSpec((height, block), lambda k: (0, offset * steps + k))

    in_specs = [pl.BlockSpec((a.shape[0], block), lambda k: (0, k)) for a in (*summed, *arrived)]
    share = rows // len(olds)
    in_specs += [old_spec(share, c) for c in old_chunks]
    in_specs += [
        pl.BlockSpec((rows, total), lambda k: (0, 0)),
        pl.BlockSpec((total, block), lambda k: (0, first + k)),
        pl.BlockSpec((1, block), lambda k: (0, first + k)),
    ]
    in_specs += [pl.BlockSpec(memory_space=pl.ANY) for _ in after]
    *new, squares = pl.pallas_call(
        kernel,
        out_shape=(
            *[jax.ShapeDtypeStruct((piece, columns), jnp.float32)] * pieces,
            jax.ShapeDtypeStruct((rows, 128), jnp.float32),
        ),
        grid=(steps,),
        in_specs=in_specs,
        out_specs=(
            *[pl.BlockSpec((piece, block), lambda k: (0, k))] * pieces,
            pl.BlockSpec((rows, 128), lambda k: (0, 0)),
        ),
        compiler_params=pltpu.CompilerParams(vmem_limit_bytes=VMEM),
        cost_estimate=light(),
        name="assemble",
    )(*summed, *arrived, *olds, projection, stored, gaps, *after)
    return new, squares


def swap_with(value, axis, size, distance):
    return lax.ppermute(value, axis, [(i, i ^ distance) for i in range(size)])


def small(kernel, shapes, *args, name="small", scalar=None, after=()):
    out = tuple(jax.ShapeDtypeStruct(x, jnp.float32) for x in shapes)
    specs = [pl.BlockSpec(memory_space=pltpu.VMEM)] * len(args)
    if scalar is not None:
        specs = [pl.BlockSpec(memory_space=pltpu.SMEM)] + specs
        args = (scalar, *args)
    used = len(args)

    def body(*refs):
        kernel(*refs[:used], *refs[used + len(after) :])

    specs += [pl.BlockSpec(memory_space=pl.ANY)] * len(after)
    args = (*args, *after)
    return pl.pallas_call(
        body,
        out_shape=out,
        in_specs=specs,
        out_specs=tuple(pl.BlockSpec(memory_space=pltpu.VMEM) for _ in out),
        compiler_params=pltpu.CompilerParams(vmem_limit_bytes=VMEM // 2),
        cost_estimate=light(),
        name=name,
    )(*args)


def total_of(*values, after=()):
    def kernel(*refs):
        acc = refs[0][...]
        for r in refs[1:-1]:
            acc = acc + r[...]
        refs[-1][...] = acc

    return small(kernel, [values[0].shape], *values, name="total", after=after)[0]


def joined(keep, near, parts, after=(), most=4096):
    rows, columns = keep.shape
    block = block_of(columns, most)
    each = near[0].shape[0]
    height = rows // parts

    def kernel(k_ref, *refs):
        ins, outs = refs[: len(near)], refs[len(near) + len(after) :]
        for i, r in enumerate(ins):
            at = i * each
            outs[at // height][at % height : at % height + each] = k_ref[at : at + each] + r[...]

    return pl.pallas_call(
        kernel,
        out_shape=tuple([jax.ShapeDtypeStruct((height, columns), jnp.float32)] * parts),
        grid=(columns // block,),
        in_specs=[pl.BlockSpec((rows, block), lambda k: (0, k))]
        + [pl.BlockSpec((each, block), lambda k: (0, k))] * len(near)
        + [pl.BlockSpec(memory_space=pl.ANY)] * len(after),
        out_specs=tuple([pl.BlockSpec((height, block), lambda k: (0, k))] * parts),
        compiler_params=pltpu.CompilerParams(vmem_limit_bytes=VMEM),
        cost_estimate=light(),
        name="joined",
    )(keep, *near, *after)


def pair_sum(value, size, between=(None, None), last=None, after=()):
    rows, columns = value.shape
    block = rows // 4
    me = jnp.reshape(lax.axis_index("pair") % 4, (1,)).astype(jnp.int32)

    def cut(m_ref, v_ref, *out):
        for d, o in enumerate(out):
            o[...] = v_ref[pl.ds(pl.multiple_of((m_ref[0] ^ d) * block, 8), block), :]

    def gather(m_ref, *refs):
        for d, r in enumerate(refs[:-1]):
            refs[-1][pl.ds(pl.multiple_of((m_ref[0] ^ d) * block, 8), block), :] = r[...]

    mine, *rest = small(cut, [(block, columns)] * 4, value, scalar=me, name="cut", after=after)
    others = [swap_with(r, "pair", size, d) for d, r in enumerate(rest, 1)]
    after = [between[0]([mine])] if between[0] else []
    total = total_of(mine, *others, after=after)
    distance = 4
    while distance < size:
        other = swap_with(total, "pair", size, distance)
        after = [between[1]([total])] if between[1] and distance == 4 else []
        total = total_of(total, other, after=after)
        distance *= 2
    every = [total] + [swap_with(total, "pair", size, d) for d in (1, 2, 3)]
    after = [last([total])] if last else []
    return small(gather, [(rows, columns)], *every, scalar=me, name="gather", after=after)[0]


def small_sum(value, size):
    if size & (size - 1):
        return lax.psum(value, "pair")
    distance = 1
    if size % 4 == 0:
        value = total_of(value, *(swap_with(value, "pair", size, d) for d in (1, 2, 3)))
        distance = 4
    while distance < size:
        value = total_of(value, swap_with(value, "pair", size, distance))
        distance *= 2
    return value


def on_device(n_pair, n_aux, factor, trials, stored, energy_gaps):
    local, aux = factor.shape
    total = stored.shape[0]
    pairs = local * n_pair
    owned = trials.shape[0]
    own_s = total // n_aux
    me = lax.axis_index("aux")
    which = (jnp.reshape(me, (1,)).astype(jnp.int32), n_aux)
    gaps = energy_gaps[None, :]
    chunks = 2
    h = owned // 2
    two = 2 * h
    kc = local // chunks
    aux_swap = functools.partial(swap_with, axis="aux", size=n_aux)
    over = functools.partial(pass_over, factor)
    wide = dict(gaps=gaps, stored=stored, which=which)

    def project(fitted):
        def part(m_ref, f_ref, w_ref, keep_ref, send_ref):
            f = jnp.concatenate(split(4.0 * f_ref[:, :aux]), axis=0)
            own = f_ref[:, aux:]
            shape = (own.shape[1], total)
            row = lax.broadcasted_iota(jnp.int32, shape, 0)
            column = lax.broadcasted_iota(jnp.int32, shape, 1)
            here = (column == row + m_ref[0] * own_s) & (row < own_s)
            here = jnp.where(here, 1.0, 0.0).astype(jnp.bfloat16)
            placed = dot(jnp.concatenate(split(own), axis=0), here, NN)
            rows = own.shape[0]
            out = dot3(f, split(w_ref[...]), NT) + placed[:rows] + placed[rows:]
            keep_ref[...] = out[:two]
            send_ref[...] = out[two:]

        def both(k_ref, t_ref, o_ref):
            o_ref[:h] = k_ref[:h] + t_ref[h:]
            o_ref[h:] = k_ref[h:] + t_ref[:h]

        keep, send = small(part, [(two, total)] * 2, fitted, crossed, scalar=which[0], name="project")
        first_part = keep
        keep = total_of(keep, aux_swap(send, distance=1))
        part_sum = small(both, [(two, total)], keep, aux_swap(keep, distance=2), name="both")[0]
        return first_part, part_sum

    everyone = []
    for g in range(2):
        own = trials[g * h : (g + 1) * h]
        everyone.append([own, aux_swap(own, distance=2)])

    def near_too(parts, token):
        parts = lax.optimization_barrier((*parts, token))[:2]
        return [*parts, *(aux_swap(p, distance=1) for p in parts)]

    (crossed,) = over(0, local, parts=[stored])
    everyone[0] = near_too(everyone[0], crossed)
    held = [None]

    def first_fit(c):
        def run(after):
            held.extend(over(c, kc, parts=everyone[0], before=held[-1], after=after, **wide))
            return held[-1]

        return run

    begins = []

    def first_way(after):
        begins.append(pair_sum(held[-1], n_pair, after=after))
        everyone[1] = near_too(everyone[1], begins[0])
        begins.append(over(0, kc, fitted=begins[0], parts=everyone[1], **wide))
        return begins[1][2]

    crossed = pair_sum(crossed, n_pair, (first_fit(0), first_fit(1)), first_way)
    one = begins[0]

    def summed(keep, send, after):
        (keep,) = joined(keep, [aux_swap(x, distance=1) for x in send], 1, after)
        return [keep], [aux_swap(keep, distance=2)]

    def new_vectors(g, c, projection, token):
        new, square = assemble(
            *sent[g][c], everyone[g][:2], (c, c), projection, stored, gaps, c, True, after=token
        )
        current[g].append(new + [aux_swap(x, distance=1) for x in new])
        squares[g] = squares[g] + square[:h]
        return new[0]

    begun, first = project(one)
    projected = [[None, None], [None, None]]
    projected[0][0] = first[:h]
    keep, send, partial = begins[1]
    sent = [[summed(keep, send, [first])], []]
    for c in range(1, chunks):
        keep, send, partial = over(
            c, kc, fitted=one, parts=everyone[1], before=partial, after=[sent[0][-1][0][0]], **wide
        )
        sent[0].append(summed(keep, send, []))
    current = [[], []]
    squares = [0.0, 0.0]
    firsts = []

    def early(g, projection, token):
        def run(after):
            firsts.append(new_vectors(g, 0, projection, [*after, *token]))
            return firsts[-1]

        return run

    two_sum = pair_sum(partial, n_pair, (None, early(0, first, [sent[0][-1][0][0]])))
    begun, second = project(two_sum)
    projected[0][1] = second[:h]

    partial, token = None, firsts[0]
    for c in range(chunks):
        keep, send, partial = over(
            c, kc, fitted=two_sum, parts=current[0][c], before=partial, after=[begun, token], **wide
        )
        token = partial
        if c + 1 < chunks:
            token = new_vectors(0, c + 1, first, [partial])
        sent[1].append(summed(keep, send, [second, token]))
        token = sent[1][-1][0][0]
    one = pair_sum(partial, n_pair, (None, early(1, second, [token])))
    begun, aux_sum = project(one)
    first = aux_sum[:h]
    projected[1][0] = first

    def last_sum(keep, send, after, split_in=1):
        near = [aux_swap(x, distance=1) for x in send]
        out = joined(keep, near, 2 * split_in, after)
        return out[:split_in], [aux_swap(x, distance=2) for x in out[split_in:]]

    last = [[], []]
    keep, send, partial = over(0, kc, fitted=one, parts=current[1][0], after=[begun, firsts[1]], **wide)
    last[0].append(last_sum(keep, send, [aux_sum]))
    for c in range(1, chunks):
        keep, send = over(c, kc, fitted=one, after=[last[0][-1][0][0]])
        last[0].append(last_sum(keep, send, []))
    for c in range(1, chunks):
        new_vectors(1, c, second, [last[0][-1][0][0]])
        (partial,) = over(c, kc, parts=current[1][c], before=partial, **wide)
    ends = [[], []]
    norms = [0.0, 0.0]

    def finish(g, c, projection, token):
        new, square = assemble(
            *last[g][c],
            current[g][c][: PIECES // 2],
            (0,) * (PIECES // 2),
            projection,
            stored,
            gaps,
            c,
            False,
            after=token,
        )
        ends[g].append(new[0])
        norms[g] = norms[g] + square
        return new[0]

    two_sum = pair_sum(
        partial,
        n_pair,
        (lambda after: finish(0, 0, first, after), lambda after: finish(0, 1, first, after)),
    )
    begun, aux_sum = project(two_sum)
    second = aux_sum[:h]
    projected[1][1] = second
    token = [begun]
    for c in range(chunks):
        keep, send = over(c, kc, fitted=two_sum, after=token, pieces=PIECES * (c + 1))
        last[1].append(last_sum(keep, send, [aux_sum], 4 if c else 1))
        token = [last[1][-1][0][0]]
    token = []
    for c in range(chunks):
        token = [finish(1, c, second, token)]

    sums = jnp.concatenate([jnp.concatenate(squares, 0), jnp.concatenate(norms, 0)], axis=1)
    sums = small_sum(sums, n_pair)
    norm = jnp.sqrt(sums[:, :1] / pairs + 1e-06)
    scale = norm * jnp.sqrt(sums[:, 128:129] / (norm * norm) / pairs + 1e-06)
    out = jnp.concatenate([jnp.concatenate(e, axis=1) for e in ends], axis=0) / scale
    first_p = jnp.concatenate(projected[0], axis=0)
    second_p = jnp.concatenate(projected[1], axis=0) / norm
    return out, jnp.stack([first_p.T, second_p.T])


def solution(mesh):
    in_specs = (P("pair", "aux"), P("aux", "pair"), P(None, "pair"), P("pair"))
    out_specs = (P("aux", "pair"), P(None, None, "aux"))
    body = functools.partial(on_device, mesh.shape["pair"], mesh.shape["aux"])
    return jax.shard_map(body, mesh=mesh, in_specs=in_specs, out_specs=out_specs, check_vma=False)
```
